32 devices in a mesh: group: 4 (over y, core), sub: 8 (over z, x).
Axes of the slice: x: 2, y: 2, z: 4, core: 2. Of those that a mesh axis runs over, the one named last changes fastest.
Arguments:
- right_side: float32 [16384, 128], P(('group', 'sub')), may hold values from -6 to 6
- mass: float32 [32, 512], P(('group', 'sub')), may hold values from 0.05 to 0.5
- block_values: float32 [16384, 512], P(('group', 'sub')), may hold values from 0.000390625 to 0.005859375
- block_cols: int32 [256, 8], P(('group', 'sub')), may hold values from 0 to 7, as said below
- face_rows: int32 [32, 64], P(('group', 'sub')), may hold values from 0 to 511, as said below
- land_rows: int32 [32, 64], P(('group', 'sub')), may hold values from 0 to 511, as said below
- face_counts: int32 [32, 8], P(('group', 'sub')), may hold values from 0 to 8, as said below
- face_weight: float32 [32, 64], P(('group', 'sub')), may hold values from 0.3 to 3
- local_factor: float32 [16384, 128], P(('group', 'sub')), may hold values from -0.25 to 0.25
- basis: float32 [2048, 512], P(('group', 'sub')), may hold values from -0.25 to 0.25
- coarse_inverse: float32 [512, 512], P('sub'), may hold values from -1 to 2.5, as said below
Outputs:
- solution_field: float32 [16384, 128], P(('group', 'sub'))
- residual: float32 [16384, 128], P(('group', 'sub'))
The draws below stay inside these ranges and needn't reach their ends.
Inputs may be any that keep to these rules, and one draw needn't show every extreme that they name: `block_cols`: for each k, the column blocks of a subdomain's 8 block rows are a permutation of 0 to 7. `face_rows`: the 64 entries of a subdomain are distinct local rows. `land_rows`: the 64 entries of a subdomain are distinct local rows. `face_counts`: every subdomain has 8 live slots toward at least one peer. `coarse_inverse`: symmetric positive definite.
All inputs are finite; a program needn't handle non-finite values.
Results may differ from the reference program's by a relative error of at most 0.0003.
Values sent between devices are 32-bit elements; how exact they have to be, the bound alone decides.
A program may use at most 64 MiB of HBM per device.

```python
import math
import jax
import jax.numpy as jnp
from jax import lax

NB = 8
BLK = 64
NNZB = 8
RHS = 128
F = 8
NC = 64
LF = 128
ITERS = 3
SUBDOMAINS = 32
ROWS_DEV = 512
ROWS = 16384
NBT = 256
NCT = 512
SLOTS = 64
N_GROUP = 4
N_SUB = 8


def draw_block_cols(key, part):
    key = jax.random.fold_in(key, 11)
    key_list = jax.random.split(key, SUBDOMAINS * NNZB)
    perms = jax.vmap(lambda single: jax.random.permutation(single, NB))(key_list)
    perms = perms.reshape(SUBDOMAINS, NNZB, NB).astype(jnp.int32)
    return jnp.swapaxes(perms, 1, 2).reshape(NBT, NNZB)


def draw_face_rows(key, part):
    key = jax.random.fold_in(key, 23)
    key_list = jax.random.split(key, SUBDOMAINS)
    chosen = jax.vmap(lambda single: jax.random.permutation(single, ROWS_DEV)[:SLOTS])(key_list)
    return chosen.astype(jnp.int32)


def draw_land_rows(key, part):
    key = jax.random.fold_in(key, 37)
    key_list = jax.random.split(key, SUBDOMAINS)
    chosen = jax.vmap(lambda single: jax.random.permutation(single, ROWS_DEV)[:SLOTS])(key_list)
    return chosen.astype(jnp.int32)


def draw_face_counts(key, part):
    key = jax.random.fold_in(key, 41)
    first, second = jax.random.split(key)
    counts = jax.random.randint(first, (SUBDOMAINS, N_SUB), 0, F + 1).astype(jnp.int32)
    fullest = jax.random.randint(second, (SUBDOMAINS,), 0, N_SUB).astype(jnp.int32)
    peers = jnp.arange(N_SUB, dtype=jnp.int32)
    return jnp.where(peers[None, :] == fullest[:, None], jnp.int32(F), counts)


def draw_coarse_inverse(key, part):
    key = jax.random.fold_in(key, 53)
    first, second = jax.random.split(key)
    noise = jnp.clip(jax.random.normal(first, (NCT, NCT), jnp.float32), -4.0, 4.0)
    sym = (noise + noise.T) * (0.3 / (2.0 * NCT) ** 0.5)
    diagonal = 1.0 + 0.5 * jax.random.uniform(second, (NCT,), jnp.float32)
    return sym + jnp.diag(diagonal)


def levels(own_key, extent, cuts, low, largest):
    factor_of, own = 1.0, jax.random.fold_in(own_key, 6)
    for position, shards_of in cuts:
        draws = jnp.exp(jax.random.uniform(jax.random.fold_in(own, position), (shards_of,), jnp.float32, low / len(cuts), largest / len(cuts)))
        factor_of = factor_of * jnp.repeat(draws, extent[position] // shards_of).reshape([-1 if axis == position else 1 for axis in range(len(extent))])
    return factor_of


def normal_values(key, shape, deviation, reach, cuts=(), kind=jnp.bfloat16):
    entries = jax.random.normal(key, shape, jnp.float32) * deviation
    if len(cuts) > 0:
        entries = levels(key, shape, cuts, -0.22, 0.18) * entries
    return jnp.clip(entries, min=-reach, max=reach).astype(kind)


def setup_inputs(seed: int = 0) -> dict:
    key_of = jax.random.split(jax.random.key(seed), 12)
    return {
        "right_side": normal_values(key_of[0], (ROWS, RHS), 1.0, 6.0, ((0, 32),), jnp.float32),
        "mass": jnp.clip(jnp.exp(math.log(0.5) - 2.3025851 * jax.random.uniform(key_of[1], (SUBDOMAINS, ROWS_DEV), jnp.float32) ** levels(key_of[1], (SUBDOMAINS, ROWS_DEV), ((0, 32),), -0.2, 0.2)), 0.05, 0.5),
        "block_values": jnp.clip(jnp.exp(math.log(0.005859375) - 2.7080502 * jax.random.uniform(key_of[2], (ROWS, NNZB * BLK), jnp.float32) ** levels(key_of[2], (ROWS, NNZB * BLK), ((0, 32),), -0.2, 0.2)), 0.000390625, 0.005859375),
        "block_cols": draw_block_cols(jax.random.fold_in(key_of[11], 71), 0),
        "face_rows": draw_face_rows(jax.random.fold_in(key_of[11], 71), 0),
        "land_rows": draw_land_rows(jax.random.fold_in(key_of[11], 71), 0),
        "face_counts": draw_face_counts(jax.random.fold_in(key_of[11], 71), 0),
        "face_weight": jnp.clip(jnp.exp(math.log(3.0) - 2.3025851 * jax.random.uniform(key_of[7], (SUBDOMAINS, SLOTS), jnp.float32) ** levels(key_of[7], (SUBDOMAINS, SLOTS), ((0, 32),), -0.2, 0.2)), 0.3, 3.0),
        "local_factor": normal_values(key_of[8], (ROWS, LF), (4 * LF) ** -0.5, 0.25, ((0, 32),), jnp.float32),
        "basis": normal_values(key_of[9], (SUBDOMAINS * NC, ROWS_DEV), ROWS_DEV ** -0.5, 0.25, ((0, 32),), jnp.float32),
        "coarse_inverse": draw_coarse_inverse(jax.random.fold_in(key_of[11], 71), 0),
    }


highest = lax.Precision.HIGHEST


def swap_peers(sent):
    shaped = sent.reshape((N_GROUP, N_SUB, N_SUB, F) + sent.shape[2:])
    turned = jnp.swapaxes(shaped, 1, 2)
    return turned.reshape((SUBDOMAINS, SLOTS) + sent.shape[2:])


def degree_one(values_dev, cols_dev, faces_dev, lands_dev, weights_dev, received_dev):
    row_total = jnp.sum(values_dev, axis=1)
    col_part = jnp.sum(values_dev.reshape(NB, BLK, NNZB * BLK), axis=1).reshape(NB * NNZB, BLK)
    col_total = jnp.zeros((NB, BLK), jnp.float32).at[cols_dev.reshape(-1)].add(col_part).reshape(ROWS_DEV)
    total = row_total + col_total
    return total.at[faces_dev].add(weights_dev).at[lands_dev].add(received_dev)


def local_one(packed):
    values_dev, cols_dev, field, faces_dev, lands_dev, weights_dev, got_out, got_back, diag_dev = packed
    values_r = values_dev.reshape(NB, BLK, NNZB * BLK)
    blocks = field.reshape(NB, BLK, RHS)
    picked = blocks[cols_dev].reshape(NB, NNZB * BLK, RHS)
    forward = jnp.einsum('rik,rkc->ric', values_r, picked, precision=highest).reshape(ROWS_DEV, RHS)
    back_terms = jnp.einsum('rik,ric->rkc', values_r, blocks, precision=highest).reshape(NB * NNZB, BLK, RHS)
    backward = jnp.zeros((NB, BLK, RHS), jnp.float32).at[cols_dev.reshape(-1)].add(back_terms).reshape(ROWS_DEV, RHS)
    coupled = jnp.zeros((ROWS_DEV, RHS), jnp.float32).at[lands_dev].add(got_out)
    coupled = coupled.at[faces_dev].add(weights_dev[:, None] * got_back)
    return diag_dev[:, None] * field - forward - backward - coupled


def reference(right_side, mass, block_values, block_cols, face_rows, land_rows, face_counts, face_weight, local_factor, basis, coarse_inverse):
    values_all = block_values.reshape(SUBDOMAINS, ROWS_DEV, NNZB * BLK)
    cols_all = block_cols.reshape(SUBDOMAINS, NB, NNZB)
    slot_ids = jnp.arange(SLOTS)
    live = (slot_ids % F)[None, :] < face_counts[:, slot_ids // F]
    weights = jnp.where(live, face_weight, jnp.float32(0.0))
    received = swap_peers(weights)
    degree = jax.vmap(degree_one)(values_all, cols_all, face_rows, land_rows, weights, received)
    diag = mass + degree
    factor_r = local_factor.reshape(SUBDOMAINS, ROWS_DEV // LF, LF, LF)
    basis_r = basis.reshape(SUBDOMAINS, NC, ROWS_DEV)

    def operate(field):
        sent_out = weights[:, :, None] * jnp.take_along_axis(field, face_rows[:, :, None], axis=1)
        sent_back = jnp.take_along_axis(field, land_rows[:, :, None], axis=1)
        got_out = swap_peers(sent_out)
        got_back = swap_peers(sent_back)
        return lax.map(local_one, (values_all, cols_all, field, face_rows, land_rows, weights, got_out, got_back, diag))

    def precondition(resid):
        jacobi = resid / diag[:, :, None]
        blocks = resid.reshape(SUBDOMAINS, ROWS_DEV // LF, LF, RHS)
        inner = jnp.einsum('dbij,dbjc->dbic', factor_r, blocks, precision=highest)
        local_part = jnp.einsum('dbji,dbjc->dbic', factor_r, inner, precision=highest).reshape(SUBDOMAINS, ROWS_DEV, RHS)
        coarse_part = jnp.einsum('dnr,drc->dnc', basis_r, resid, precision=highest)
        coarse_rhs = jnp.sum(coarse_part.reshape(N_GROUP, NCT, RHS), axis=0)
        solved = jnp.dot(coarse_inverse, coarse_rhs, precision=highest).reshape(N_SUB, NC, RHS)
        spread = jnp.broadcast_to(solved[None], (N_GROUP, N_SUB, NC, RHS)).reshape(SUBDOMAINS, NC, RHS)
        coarse_term = jnp.einsum('dnr,dnc->drc', basis_r, spread, precision=highest)
        return jacobi + local_part + coarse_term

    resid = right_side.reshape(SUBDOMAINS, ROWS_DEV, RHS)
    solution = jnp.zeros_like(resid)
    zvalue = precondition(resid)
    direction = zvalue
    gamma = jnp.sum(resid * zvalue, axis=(0, 1))
    for iteration in range(ITERS):
        image = operate(direction)
        alpha = gamma / jnp.sum(direction * image, axis=(0, 1))
        solution = solution + alpha * direction
        resid = resid - alpha * image
        if iteration + 1 < ITERS:
            zvalue = precondition(resid)
            gamma_new = jnp.sum(resid * zvalue, axis=(0, 1))
            direction = zvalue + (gamma_new / gamma) * direction
            gamma = gamma_new
    return solution.reshape(ROWS, RHS), resid.reshape(ROWS, RHS)
```

```python
import functools

import jax
import jax.numpy as jnp
from jax import lax
from jax.experimental import pallas as pl
from jax.experimental.pallas import tpu as pltpu
from jax.sharding import PartitionSpec as P

HIGHEST = lax.Precision.HIGHEST
MESH = pl.DeviceIdType.MESH
LANES = 128
SUBLANES = 8


def mm(a, b):
    return jnp.dot(a, b, precision=HIGHEST, preferred_element_type=jnp.float32)


def stack_dots(rows):
    pad = SUBLANES - len(rows)
    return jnp.concatenate(rows + [jnp.zeros((pad, rows[0].shape[1]), jnp.float32)], axis=0)


def column_dot(a, b):
    return jnp.sum(a * b, axis=0, keepdims=True)


def kernel(
    n_group,
    n_sub,
    rs_ref,
    mass_ref,
    values_ref,
    cols_ref,
    faces_ref,
    lands_ref,
    counts_ref,
    fweight_ref,
    factor_ref,
    basis_ref,
    coarse_ref,
    x_ref,
    r_ref,
    dense,
    near,
    inv_diag,
    diag,
    basis_t,
    select,
    spread,
    extend_out,
    extend_in,
    weight_out,
    weight_in,
    group_buf,
    sub_buf,
    face_out,
    face_in,
    group_dots,
    sub_dots,
    send_sem,
    recv_sem,
):
    me_g = lax.axis_index("group")
    me_s = lax.axis_index("sub")
    n_rows, n_rhs = rs_ref.shape
    n_slots = faces_ref.shape[1]
    per_peer = n_slots // n_sub
    n_blocks, n_stored = cols_ref.shape
    block_rows = n_rows // n_blocks
    n_coarse = basis_ref.shape[0]
    total_coarse = coarse_ref.shape[1]
    factor_rows = factor_ref.shape[1]
    n_factors = n_rows // factor_rows

    barrier = pltpu.get_barrier_semaphore()
    for step in range(1, n_group):
        peer = lax.rem(me_g + step, n_group)
        pl.semaphore_signal(barrier, inc=1, device_id=(peer, me_s), device_id_type=MESH)
    for step in range(1, n_sub):
        peer = lax.rem(me_s + step, n_sub)
        pl.semaphore_signal(barrier, inc=1, device_id=(me_g, peer), device_id_type=MESH)

    pending = []

    def over_sub(channel, src_of, dst):
        for step in range(1, n_sub):
            peer = lax.rem(me_s + step, n_sub)
            pltpu.make_async_remote_copy(
                src_ref=src_of(peer),
                dst_ref=dst,
                send_sem=send_sem.at[channel],
                recv_sem=recv_sem.at[channel],
                device_id=(me_g, peer),
                device_id_type=MESH,
            ).start()

    def over_group(channel, src, dst):
        for step in range(1, n_group):
            peer = lax.rem(me_g + step, n_group)
            pltpu.make_async_remote_copy(
                src_ref=src,
                dst_ref=dst,
                send_sem=send_sem.at[channel],
                recv_sem=recv_sem.at[channel],
                device_id=(peer, me_s),
                device_id_type=MESH,
            ).start()

    def arrive(channel, buf, count):
        if count > 0:
            part = buf.at[pl.ds(0, count)]
            pltpu.make_async_copy(part, part, recv_sem.at[channel]).wait()
            pending.append((channel, buf, count))

    slot = lax.broadcasted_iota(jnp.int32, (1, n_slots), 1)
    count_row = jnp.zeros((1, n_slots), jnp.int32)
    for p in range(n_sub):
        count_row = jnp.where(slot // per_peer == p, counts_ref[0, p], count_row)
    weights = jnp.where(slot % per_peer < count_row, fweight_ref[...], jnp.float32(0.0))
    row_ids = lax.broadcasted_iota(jnp.int32, (n_rows, n_slots), 0)
    face_hot = jnp.where(row_ids == faces_ref[...], weights, jnp.float32(0.0))
    land_hot = jnp.where(row_ids == lands_ref[...], jnp.float32(1.0), jnp.float32(0.0))
    spread[:, :n_slots] = land_hot
    spread[:, n_slots:] = face_hot
    select[:n_slots, :] = face_hot.T
    select[n_slots:, :] = land_hot.T

    weight_out[...] = mm(
        select[:n_slots, :], jnp.ones((n_rows, n_rhs), jnp.float32)
    ).reshape(n_sub, per_peer, n_rhs)
    weight_in[pl.ds(me_s, 1)] = weight_out[pl.ds(me_s, 1)]
    resid = rs_ref[...]
    group_buf[0, me_g] = jnp.concatenate(
        [mm(basis_ref[...], resid), jnp.zeros((SUBLANES, n_rhs), jnp.float32)], axis=0
    )

    pl.semaphore_wait(barrier, n_group - 1 + n_sub - 1)

    over_group(2, group_buf.at[0, me_g], group_buf.at[0, me_g])
    over_sub(0, lambda peer: weight_out.at[peer], weight_in.at[me_s])

    basis_t[...] = basis_ref[...].T
    reach = mm(mm(select[...], basis_t[...]), coarse_ref[...])
    extend_out[:, :per_peer, :] = reach[:n_slots].reshape(n_sub, per_peer, total_coarse)
    extend_out[:, per_peer:, :] = reach[n_slots:].reshape(n_sub, per_peer, total_coarse)
    extend_in[pl.ds(me_s, 1)] = extend_out[pl.ds(me_s, 1)]

    def gather_group(phase):
        arrive(2 + phase, group_buf.at[phase], n_group - 1)
        total = group_buf[phase, 0]
        for g in range(1, n_group):
            total = total + group_buf[phase, g]
        sub_buf[phase, me_s] = total
        over_sub(6 + phase, lambda peer: sub_buf.at[phase, me_s], sub_buf.at[phase, me_s])

    gather_group(0)
    over_sub(1, lambda peer: extend_out.at[peer], extend_in.at[me_s])

    lane = lax.broadcasted_iota(jnp.int32, (1, LANES), 1)
    high = jnp.where(lane >= block_rows, 1, 0)
    n_tiles = n_rows // LANES
    stored_tiles = n_stored * block_rows // LANES
    for b in range(n_blocks):
        rows = slice(b * block_rows, (b + 1) * block_rows)
        sums = [jnp.zeros((block_rows, LANES), jnp.float32) for _ in range(n_tiles)]
        for t in range(stored_tiles):
            tile = values_ref[rows, t * LANES : (t + 1) * LANES]
            turned = pltpu.roll(tile, block_rows, 1)
            first, second = cols_ref[b, 2 * t], cols_ref[b, 2 * t + 1]
            straight_cols = jnp.where(high == 0, first, second)
            turned_cols = jnp.where(high == 0, second, first)
            for u in range(n_tiles):
                target = 2 * u + high
                sums[u] = (
                    sums[u]
                    + jnp.where(straight_cols == target, tile, jnp.float32(0.0))
                    + jnp.where(turned_cols == target, turned, jnp.float32(0.0))
                )
        for u in range(n_tiles):
            dense[rows, u * LANES : (u + 1) * LANES] = sums[u]
    dense[...] = dense[...] + dense[...].T

    for i in range(n_factors):
        rows = slice(i * factor_rows, (i + 1) * factor_rows)
        part = factor_ref[rows, :]
        near[rows, :] = mm(part.T, part)

    degree = mm(dense[...], jnp.ones((n_rows, n_rhs), jnp.float32))
    mass_col = jnp.broadcast_to(mass_ref[...], (n_rhs, n_rows)).T
    arrive(0, weight_in, n_sub - 1)
    degree = degree + mm(
        spread[...],
        jnp.concatenate(
            [
                weight_in[...].reshape(n_slots, n_rhs),
                jnp.ones((n_slots, n_rhs), jnp.float32),
            ],
            axis=0,
        ),
    )
    diag[...] = mass_col + degree
    inv_diag[...] = 1.0 / diag[...]

    def send_coarse(phase, field, dots):
        group_buf[phase, me_g] = jnp.concatenate([mm(basis_ref[...], field), dots], axis=0)
        over_group(2 + phase, group_buf.at[phase, me_g], group_buf.at[phase, me_g])

    def send_local(phase, field):
        parts = []
        for i in range(n_factors):
            rows = slice(i * factor_rows, (i + 1) * factor_rows)
            parts.append(mm(near[rows, :], field[rows, :]))
        local_part = field * inv_diag[...] + jnp.concatenate(parts, axis=0)
        picked = mm(select[...], local_part)
        face_out[phase, :, :per_peer, :] = picked[:n_slots].reshape(n_sub, per_peer, n_rhs)
        face_out[phase, :, per_peer:, :] = picked[n_slots:].reshape(n_sub, per_peer, n_rhs)
        face_in[phase, me_s] = face_out[phase, me_s]
        over_sub(10 + phase, lambda peer: face_out.at[phase, peer], face_in.at[phase, me_s])
        return local_part

    def receive(phase, local_part):
        arrive(6 + phase, sub_buf.at[phase], n_sub - 1)
        whole = sub_buf[phase, :, :n_coarse, :].reshape(total_coarse, n_rhs)
        dots = jnp.sum(sub_buf[phase, :, n_coarse:, :], axis=0)
        if phase == 0:
            arrive(1, extend_in, n_sub - 1)
        field = local_part + mm(basis_t[...], mm(coarse_ref[...], whole))
        far = mm(extend_in[...].reshape(2 * n_slots, total_coarse), whole)
        arrive(10 + phase, face_in.at[phase], n_sub - 1)
        far = far.reshape(n_sub, 2 * per_peer, n_rhs) + face_in[phase]
        far = jnp.concatenate(
            [
                far[:, :per_peer, :].reshape(n_slots, n_rhs),
                far[:, per_peer:, :].reshape(n_slots, n_rhs),
            ],
            axis=0,
        )
        return field, far, dots

    def operate(field, far):
        return diag[...] * field - mm(dense[...], field) - mm(spread[...], far)

    local_part = send_local(0, resid)
    z, z_far, _ = receive(0, local_part)
    image = operate(z, z_far)
    send_coarse(1, image, stack_dots([column_dot(resid, z), column_dot(z, image)]))
    local_part = send_local(1, image)
    gather_group(1)
    m_image, m_far, dots = receive(1, local_part)
    gamma, bent = dots[0:1], dots[1:2]
    alpha = gamma / bent
    direction = z
    answer = alpha * direction
    resid = resid - alpha * image
    z = z - alpha * m_image
    z_far = z_far - alpha * m_far
    z_image = operate(z, z_far)
    send_coarse(
        2,
        z_image,
        stack_dots([column_dot(resid, z), column_dot(z, z_image), column_dot(z, image)]),
    )
    local_part = send_local(2, z_image)
    gather_group(2)
    m_z_image, m_z_far, dots = receive(2, local_part)
    beta = dots[0:1] / gamma
    gamma = dots[0:1]
    bent = dots[1:2] + beta * (2.0 * dots[2:3] + beta * bent)
    alpha = gamma / bent
    direction = z + beta * direction
    image = z_image + beta * image
    answer = answer + alpha * direction
    resid = resid - alpha * image
    z = z - alpha * (m_z_image + beta * m_image)
    z_far = z_far - alpha * (m_z_far + beta * m_far)
    z_image = operate(z, z_far)
    group_dots[me_g] = stack_dots(
        [column_dot(resid, z), column_dot(z, z_image), column_dot(z, image)]
    )
    over_group(5, group_dots.at[me_g], group_dots.at[me_g])
    arrive(5, group_dots, n_group - 1)
    sub_dots[me_s] = jnp.sum(group_dots[...], axis=0)
    over_sub(9, lambda peer: sub_dots.at[me_s], sub_dots.at[me_s])
    arrive(9, sub_dots, n_sub - 1)
    dots = jnp.sum(sub_dots[...], axis=0)
    beta = dots[0:1] / gamma
    gamma = dots[0:1]
    bent = dots[1:2] + beta * (2.0 * dots[2:3] + beta * bent)
    alpha = gamma / bent
    x_ref[...] = answer + alpha * (z + beta * direction)
    r_ref[...] = resid - alpha * (z_image + beta * image)

    for channel, buf, count in pending:
        part = buf.at[pl.ds(0, count)]
        pltpu.make_async_copy(part, part, send_sem.at[channel]).wait()


def local(n_group, n_sub, *args):
    right_side, block_cols, face_rows = args[0], args[3], args[4]
    basis, coarse_inverse = args[9], args[10]
    n_rows, n_rhs = right_side.shape
    n_slots = face_rows.shape[1]
    per_peer = n_slots // n_sub
    n_coarse = basis.shape[0]
    total_coarse = coarse_inverse.shape[1]
    factor_rows = args[8].shape[1]
    f32 = jnp.float32
    vmem = pl.BlockSpec(memory_space=pltpu.VMEM)
    smem = pl.BlockSpec(memory_space=pltpu.SMEM)
    in_specs = [vmem, vmem, vmem, smem, vmem, vmem, smem, vmem, vmem, vmem, vmem]
    message = n_coarse + SUBLANES
    scratch = [
        pltpu.VMEM((n_rows, n_rows), f32),
        pltpu.VMEM((n_rows, factor_rows), f32),
        pltpu.VMEM((n_rows, n_rhs), f32),
        pltpu.VMEM((n_rows, n_rhs), f32),
        pltpu.VMEM((n_rows, n_coarse), f32),
        pltpu.VMEM((2 * n_slots, n_rows), f32),
        pltpu.VMEM((n_rows, 2 * n_slots), f32),
        pltpu.VMEM((n_sub, 2 * per_peer, total_coarse), f32),
        pltpu.VMEM((n_sub, 2 * per_peer, total_coarse), f32),
        pltpu.VMEM((n_sub, per_peer, n_rhs), f32),
        pltpu.VMEM((n_sub, per_peer, n_rhs), f32),
        pltpu.VMEM((3, n_group, message, n_rhs), f32),
        pltpu.VMEM((3, n_sub, message, n_rhs), f32),
        pltpu.VMEM((3, n_sub, 2 * per_peer, n_rhs), f32),
        pltpu.VMEM((3, n_sub, 2 * per_peer, n_rhs), f32),
        pltpu.VMEM((n_group, SUBLANES, n_rhs), f32),
        pltpu.VMEM((n_sub, SUBLANES, n_rhs), f32),
        pltpu.SemaphoreType.DMA((13,)),
        pltpu.SemaphoreType.DMA((13,)),
    ]
    field = jax.ShapeDtypeStruct((n_rows, n_rhs), f32)
    return pl.pallas_call(
        functools.partial(kernel, n_group, n_sub),
        out_shape=(field, field),
        in_specs=in_specs,
        out_specs=(vmem, vmem),
        scratch_shapes=scratch,
        compiler_params=pltpu.CompilerParams(
            collective_id=0, has_side_effects=True, vmem_limit_bytes=48 * 1024 * 1024
        ),
    )(*args)


def solution(mesh):
    n_group, n_sub = mesh.shape["group"], mesh.shape["sub"]
    rows = P(("group", "sub"), None)
    return jax.shard_map(
        functools.partial(local, n_group, n_sub),
        mesh=mesh,
        in_specs=(rows,) * 10 + (P("sub", None),),
        out_specs=(rows, rows),
        check_vma=False,
    )
```

```python
import functools

import jax
import jax.numpy as jnp
from jax import lax
from jax.experimental import pallas as pl
from jax.experimental.pallas import tpu as pltpu
from jax.sharding import PartitionSpec as P

HIGHEST = lax.Precision.HIGHEST
MESH = pl.DeviceIdType.MESH
LANES = 128
SUBLANES = 8


def mm(a, b):
    return jnp.dot(a, b, precision=HIGHEST, preferred_element_type=jnp.float32)


def stack_dots(rows):
    pad = SUBLANES - len(rows)
    return jnp.concatenate(rows + [jnp.zeros((pad, rows[0].shape[1]), jnp.float32)], axis=0)


def column_dot(a, b):
    return jnp.sum(a * b, axis=0, keepdims=True)


def split(x):
    high = x.astype(jnp.bfloat16)
    low = (x - high.astype(jnp.float32)).astype(jnp.bfloat16)
    return high, low


def keep(pair_ref, x, rows=slice(None)):
    high, low = split(x)
    pair_ref[0, rows] = high
    pair_ref[1, rows] = low


def mm3(pair_ref, b, rows=slice(None)):
    high, low = b
    n = high.shape[1]
    wide = jnp.dot(
        pair_ref[0, rows], jnp.concatenate([high, low], axis=1), preferred_element_type=jnp.float32
    )
    cross = jnp.dot(pair_ref[1, rows], high, preferred_element_type=jnp.float32)
    return wide[:, :n] + (wide[:, n:] + cross)


N_IN = 11


def kernel(n_group, n_sub, *refs):
    hbm = refs[:N_IN]
    x_ref, r_ref = refs[N_IN : N_IN + 2]
    held = refs[N_IN + 2 : 2 * N_IN + 2]
    (
        dense,
        dense_pair,
        near_pair,
        inv_diag,
        diag,
        basis_pair,
        basis_t_pair,
        select_pair,
        spread_pair,
        solve_pair,
        extend_out,
        extend_in,
        weight_out,
        weight_in,
        group_out,
        group_buf,
        sub_buf,
        face_out,
        face_in,
        group_dots,
        sub_dots,
        load_sem,
        send_sem,
        recv_sem,
        step_sem,
    ) = refs[2 * N_IN + 2 :]
    (
        rs_ref,
        mass_ref,
        values_ref,
        cols_ref,
        faces_ref,
        lands_ref,
        counts_ref,
        fweight_ref,
        factor_ref,
        basis_ref,
        coarse_ref,
    ) = held

    def load(i):
        return pltpu.make_async_copy(hbm[i], held[i], load_sem.at[i])

    for i in (9, 0, 4, 5, 6, 7, 10, 2, 3, 8, 1):
        load(i).start()

    me_g = lax.axis_index("group")
    me_s = lax.axis_index("sub")
    core = lax.rem(me_g, 2)
    sibling = me_g + 1 - 2 * core
    n_rows, n_rhs = rs_ref.shape
    n_slots = faces_ref.shape[1]
    per_peer = n_slots // n_sub
    n_blocks, n_stored = cols_ref.shape
    block_rows = n_rows // n_blocks
    n_coarse = basis_ref.shape[0]
    half = n_coarse // 2
    total_coarse = coarse_ref.shape[1]
    factor_rows = factor_ref.shape[1]
    n_factors = n_rows // factor_rows

    barrier = pltpu.get_barrier_semaphore()
    for step in range(1, n_group):
        peer = lax.rem(me_g + step, n_group)
        pl.semaphore_signal(barrier, inc=1, device_id=(peer, me_s), device_id_type=MESH)
    for step in range(1, n_sub):
        peer = lax.rem(me_s + step, n_sub)
        pl.semaphore_signal(barrier, inc=1, device_id=(me_g, peer), device_id_type=MESH)

    sent = []

    def send(src, dst, channel, arrived, peer):
        pltpu.make_async_remote_copy(
            src_ref=src,
            dst_ref=dst,
            send_sem=send_sem.at[channel],
            recv_sem=arrived,
            device_id=peer,
            device_id_type=MESH,
        ).start()

    def over_sub(channel, src_of, dst, arrived_of=None):
        for step in range(1, n_sub):
            peer = lax.rem(me_s + step, n_sub)
            arrived = recv_sem.at[channel] if arrived_of is None else arrived_of(step)
            send(src_of(peer), dst, channel, arrived, (me_g, peer))

    def over_group(channel, src_of, dst):
        for step in range(1, n_group):
            peer = lax.rem(me_g + step, n_group)
            send(src_of(peer), dst, channel, recv_sem.at[channel], (peer, me_s))

    def arrive(channel, part):
        pltpu.make_async_copy(part, part, recv_sem.at[channel]).wait()
        sent.append((channel, part))

    def send_coarse(phase, part, dots):
        group_out[phase, 0] = jnp.concatenate([part[:half], dots], axis=0)
        group_out[phase, 1] = jnp.concatenate([part[half:], dots], axis=0)
        group_buf[phase, me_g] = group_out[phase, core]
        if phase == 0:
            pl.semaphore_wait(barrier, n_group - 1 + n_sub - 1)
        over_group(
            2 + phase,
            lambda peer: group_out.at[phase, lax.rem(peer, 2)],
            group_buf.at[phase, me_g],
        )

    load(9).wait()
    load(0).wait()
    resid = rs_ref[...]
    send_coarse(0, mm(basis_ref[...], resid), jnp.zeros((SUBLANES, n_rhs), jnp.float32))

    for i in (4, 5, 6, 7):
        load(i).wait()
    slot = lax.broadcasted_iota(jnp.int32, (1, n_slots), 1)
    slot_peer = lax.broadcasted_iota(jnp.int32, (n_sub, n_slots), 1) // per_peer
    peer_ids = lax.broadcasted_iota(jnp.int32, (n_sub, n_slots), 0)
    of_peer = jnp.where(slot_peer == peer_ids, jnp.float32(1.0), jnp.float32(0.0))
    count_row = mm(
        jnp.broadcast_to(counts_ref[...].astype(jnp.float32), (SUBLANES, n_sub)), of_peer
    )[0:1]
    in_peer = (slot % per_peer).astype(jnp.float32)
    weights = jnp.where(in_peer < count_row - 0.5, fweight_ref[...], jnp.float32(0.0))
    row_ids = lax.broadcasted_iota(jnp.int32, (n_rows, n_slots), 0)
    face_hot = jnp.where(row_ids == faces_ref[...], weights, jnp.float32(0.0))
    land_hot = jnp.where(row_ids == lands_ref[...], jnp.float32(1.0), jnp.float32(0.0))
    spread = jnp.concatenate([land_hot, face_hot], axis=1)
    keep(spread_pair, spread)
    select = jnp.concatenate([face_hot, land_hot], axis=1).T
    keep(select_pair, select)

    weight_out[...] = mm(
        select[:n_slots, :], jnp.ones((n_rows, n_rhs), jnp.float32)
    ).reshape(n_sub, per_peer, n_rhs)
    weight_in[pl.ds(me_s, 1)] = weight_out[pl.ds(me_s, 1)]
    over_sub(0, lambda peer: weight_out.at[peer], weight_in.at[me_s])

    def gather_group(phase):
        arrive(2 + phase, group_buf.at[phase, pl.ds(0, n_group - 1)])
        total = group_buf[phase, 0]
        for g in range(1, n_group):
            total = total + group_buf[phase, g]
        sub_buf[phase, core, me_s] = total
        mine = sub_buf.at[phase, core, me_s]
        over_sub(6 + phase, lambda peer: mine, mine, lambda step: step_sem.at[phase, step])
        forward(phase, me_s)

    def forward(phase, slot_of):
        part = sub_buf.at[phase, core, slot_of, pl.ds(0, half)]
        send(part, part, 13 + phase, recv_sem.at[13 + phase], (sibling, me_s))

    gather_group(0)

    load(10).wait()
    basis_t = basis_ref[...].T
    keep(basis_t_pair, basis_t)
    keep(basis_pair, basis_ref[...])
    keep(solve_pair, coarse_ref[...], slice(0, n_coarse))
    reach = mm(mm(select, basis_t), coarse_ref[...])
    extend_out[:, :per_peer, :] = reach[:n_slots].reshape(n_sub, per_peer, total_coarse)
    extend_out[:, per_peer:, :] = reach[n_slots:].reshape(n_sub, per_peer, total_coarse)
    extend_in[pl.ds(me_s, 1)] = extend_out[pl.ds(me_s, 1)]
    over_sub(1, lambda peer: extend_out.at[peer], extend_in.at[me_s])

    load(2).wait()
    load(3).wait()
    n_tiles = n_rows // LANES
    stored = n_stored * block_rows
    stored_tiles = stored // LANES
    stored_ids = lax.broadcasted_iota(jnp.int32, (n_stored, stored), 0)
    lane_block = lax.broadcasted_iota(jnp.int32, (n_stored, stored), 1) // block_rows
    of_stored = jnp.where(stored_ids == lane_block, jnp.float32(1.0), jnp.float32(0.0))
    wide_cols = mm(cols_ref[...].astype(jnp.float32), of_stored)
    high = lax.broadcasted_iota(jnp.int32, (1, LANES), 1) // block_rows
    for b in range(n_blocks):
        rows = slice(b * block_rows, (b + 1) * block_rows)
        sums = [jnp.zeros((block_rows, LANES), jnp.float32) for _ in range(n_tiles)]
        for t in range(stored_tiles):
            tile = values_ref[rows, t * LANES : (t + 1) * LANES]
            turned = pltpu.roll(tile, block_rows, 1)
            straight_cols = wide_cols[b : b + 1, t * LANES : (t + 1) * LANES]
            turned_cols = pltpu.roll(straight_cols, block_rows, 1)
            for u in range(n_tiles):
                target = (2 * u + high).astype(jnp.float32)
                straight = jnp.abs(straight_cols - target) < 0.5
                swapped = jnp.abs(turned_cols - target) < 0.5
                sums[u] = (
                    sums[u]
                    + jnp.where(straight, tile, jnp.float32(0.0))
                    + jnp.where(swapped, turned, jnp.float32(0.0))
                )
        for u in range(n_tiles):
            dense[rows, u * LANES : (u + 1) * LANES] = sums[u]
    both = dense[...] + dense[...].T
    keep(dense_pair, both)
    degree = mm(both, jnp.ones((n_rows, n_rhs), jnp.float32))

    load(8).wait()
    for i in range(n_factors):
        rows = slice(i * factor_rows, (i + 1) * factor_rows)
        part = factor_ref[rows, :]
        keep(near_pair, mm(part.T, part), rows)

    load(1).wait()
    mass_col = jnp.broadcast_to(mass_ref[...], (n_rhs, n_rows)).T
    arrive(0, weight_in.at[pl.ds(0, n_sub - 1)])
    degree = degree + mm(
        spread,
        jnp.concatenate(
            [
                weight_in[...].reshape(n_slots, n_rhs),
                jnp.ones((n_slots, n_rhs), jnp.float32),
            ],
            axis=0,
        ),
    )
    diag[...] = mass_col + degree
    inv_diag[...] = 1.0 / diag[...]

    def send_local(phase, field, pair):
        parts = []
        for i in range(n_factors):
            rows = slice(i * factor_rows, (i + 1) * factor_rows)
            parts.append(mm3(near_pair, (pair[0][rows], pair[1][rows]), rows))
        local_part = field * inv_diag[...] + jnp.concatenate(parts, axis=0)
        picked = mm3(select_pair, split(local_part))
        face_out[phase, :, :per_peer, :] = picked[:n_slots].reshape(n_sub, per_peer, n_rhs)
        face_out[phase, :, per_peer:, :] = picked[n_slots:].reshape(n_sub, per_peer, n_rhs)
        face_in[phase, me_s] = face_out[phase, me_s]
        over_sub(10 + phase, lambda peer: face_out.at[phase, peer], face_in.at[phase, me_s])
        return local_part

    def receive(phase, local_part):
        for step in range(1, n_sub):
            origin = lax.rem(me_s + n_sub - step, n_sub)
            part = sub_buf.at[phase, core, origin]
            pltpu.make_async_copy(part, part, step_sem.at[phase, step]).wait()
            forward(phase, origin)
        dots = jnp.sum(sub_buf[phase, core, :, half:, :], axis=0)
        if phase == 0:
            arrive(1, extend_in.at[pl.ds(0, n_sub - 1)])
            keep(
                solve_pair,
                extend_in[...].reshape(2 * n_slots, total_coarse),
                slice(n_coarse, n_coarse + 2 * n_slots),
            )
        sent.append((6 + phase, sub_buf.at[phase, 0, pl.ds(0, n_sub - 1)]))
        arrive(13 + phase, sub_buf.at[phase, 0, :, pl.ds(0, half)])
        whole = jnp.concatenate(
            [sub_buf[phase, 0, :, :half, :], sub_buf[phase, 1, :, :half, :]], axis=1
        ).reshape(total_coarse, n_rhs)
        solved = mm3(solve_pair, split(whole))
        field = local_part + mm3(basis_t_pair, split(solved[:n_coarse]))
        arrive(10 + phase, face_in.at[phase, pl.ds(0, n_sub - 1)])
        far = solved[n_coarse:].reshape(n_sub, 2 * per_peer, n_rhs) + face_in[phase]
        far = jnp.concatenate(
            [
                far[:, :per_peer, :].reshape(n_slots, n_rhs),
                far[:, per_peer:, :].reshape(n_slots, n_rhs),
            ],
            axis=0,
        )
        return field, far, dots

    def operate(field, far):
        pair = split(field)
        held_field = pair[0].astype(jnp.float32) + pair[1].astype(jnp.float32)
        return diag[...] * held_field - mm3(dense_pair, pair) - mm3(spread_pair, split(far))

    local_part = send_local(0, resid, split(resid))
    z, z_far, _ = receive(0, local_part)
    image = operate(z, z_far)
    pair = split(image)
    send_coarse(
        1, mm3(basis_pair, pair), stack_dots([column_dot(resid, z), column_dot(z, image)])
    )
    local_part = send_local(1, image, pair)
    gather_group(1)
    m_image, m_far, dots = receive(1, local_part)
    gamma, bent = dots[0:1], dots[1:2]
    alpha = gamma / bent
    direction = z
    answer = alpha * direction
    resid = resid - alpha * image
    z = z - alpha * m_image
    z_far = z_far - alpha * m_far
    z_image = operate(z, z_far)
    pair = split(z_image)
    send_coarse(
        2,
        mm3(basis_pair, pair),
        stack_dots([column_dot(resid, z), column_dot(z, z_image), column_dot(z, image)]),
    )
    local_part = send_local(2, z_image, pair)
    gather_group(2)
    m_z_image, m_z_far, dots = receive(2, local_part)
    beta = dots[0:1] / gamma
    gamma = dots[0:1]
    bent = dots[1:2] + beta * (2.0 * dots[2:3] + beta * bent)
    alpha = gamma / bent
    direction = z + beta * direction
    image = z_image + beta * image
    answer = answer + alpha * direction
    resid = resid - alpha * image
    z = z - alpha * (m_z_image + beta * m_image)
    z_far = z_far - alpha * (m_z_far + beta * m_far)
    z_image = operate(z, z_far)
    group_dots[me_g] = stack_dots(
        [column_dot(resid, z), column_dot(z, z_image), column_dot(z, image)]
    )
    over_group(5, lambda peer: group_dots.at[me_g], group_dots.at[me_g])
    arrive(5, group_dots.at[pl.ds(0, n_group - 1)])
    sub_dots[me_s] = jnp.sum(group_dots[...], axis=0)
    over_sub(9, lambda peer: sub_dots.at[me_s], sub_dots.at[me_s])
    arrive(9, sub_dots.at[pl.ds(0, n_sub - 1)])
    dots = jnp.sum(sub_dots[...], axis=0)
    beta = dots[0:1] / gamma
    gamma = dots[0:1]
    bent = dots[1:2] + beta * (2.0 * dots[2:3] + beta * bent)
    alpha = gamma / bent
    x_ref[...] = answer + alpha * (z + beta * direction)
    r_ref[...] = resid - alpha * (z_image + beta * image)

    for channel, part in sent:
        pltpu.make_async_copy(part, part, send_sem.at[channel]).wait()


def local(n_group, n_sub, *args):
    right_side, face_rows = args[0], args[4]
    basis, coarse_inverse = args[9], args[10]
    n_rows, n_rhs = right_side.shape
    n_slots = face_rows.shape[1]
    per_peer = n_slots // n_sub
    n_coarse = basis.shape[0]
    total_coarse = coarse_inverse.shape[1]
    factor_rows = args[8].shape[1]
    f32 = jnp.float32
    bf16 = jnp.bfloat16
    vmem = pl.BlockSpec(memory_space=pltpu.VMEM)
    message = n_coarse // 2 + SUBLANES
    scratch = [pltpu.VMEM(arg.shape, arg.dtype) for arg in args]
    scratch += [
        pltpu.VMEM((n_rows, n_rows), f32),
        pltpu.VMEM((2, n_rows, n_rows), bf16),
        pltpu.VMEM((2, n_rows, factor_rows), bf16),
        pltpu.VMEM((n_rows, n_rhs), f32),
        pltpu.VMEM((n_rows, n_rhs), f32),
        pltpu.VMEM((2, n_coarse, n_rows), bf16),
        pltpu.VMEM((2, n_rows, n_coarse), bf16),
        pltpu.VMEM((2, 2 * n_slots, n_rows), bf16),
        pltpu.VMEM((2, n_rows, 2 * n_slots), bf16),
        pltpu.VMEM((2, n_coarse + 2 * n_slots, total_coarse), bf16),
        pltpu.VMEM((n_sub, 2 * per_peer, total_coarse), f32),
        pltpu.VMEM((n_sub, 2 * per_peer, total_coarse), f32),
        pltpu.VMEM((n_sub, per_peer, n_rhs), f32),
        pltpu.VMEM((n_sub, per_peer, n_rhs), f32),
        pltpu.VMEM((3, 2, message, n_rhs), f32),
        pltpu.VMEM((3, n_group, message, n_rhs), f32),
        pltpu.VMEM((3, 2, n_sub, message, n_rhs), f32),
        pltpu.VMEM((3, n_sub, 2 * per_peer, n_rhs), f32),
        pltpu.VMEM((3, n_sub, 2 * per_peer, n_rhs), f32),
        pltpu.VMEM((n_group, SUBLANES, n_rhs), f32),
        pltpu.VMEM((n_sub, SUBLANES, n_rhs), f32),
        pltpu.SemaphoreType.DMA((N_IN,)),
        pltpu.SemaphoreType.DMA((16,)),
        pltpu.SemaphoreType.DMA((16,)),
        pltpu.SemaphoreType.DMA((3, n_sub)),
    ]
    field = jax.ShapeDtypeStruct((n_rows, n_rhs), f32)
    return pl.pallas_call(
        functools.partial(kernel, n_group, n_sub),
        out_shape=(field, field),
        in_specs=[pl.BlockSpec(memory_space=pl.ANY)] * N_IN,
        out_specs=(vmem, vmem),
        scratch_shapes=scratch,
        compiler_params=pltpu.CompilerParams(
            collective_id=0, has_side_effects=True, vmem_limit_bytes=56 * 1024 * 1024
        ),
    )(*args)


def solution(mesh):
    n_group, n_sub = mesh.shape["group"], mesh.shape["sub"]
    rows = P(("group", "sub"), None)
    return jax.shard_map(
        functools.partial(local, n_group, n_sub),
        mesh=mesh,
        in_specs=(rows,) * 10 + (P("sub", None),),
        out_specs=(rows, rows),
        check_vma=False,
    )
```

```python
import functools

import jax
import jax.numpy as jnp
from jax import lax
from jax.experimental import pallas as pl
from jax.experimental.pallas import tpu as pltpu
from jax.sharding import PartitionSpec as P

HIGHEST = lax.Precision.HIGHEST
MESH = pl.DeviceIdType.MESH
LANES = 128
SUBLANES = 8


def mm(a, b):
    return jnp.dot(a, b, precision=HIGHEST, preferred_element_type=jnp.float32)


def stack_dots(rows):
    pad = SUBLANES - len(rows)
    return jnp.concatenate(rows + [jnp.zeros((pad, rows[0].shape[1]), jnp.float32)], axis=0)


def column_dot(a, b):
    return jnp.sum(a * b, axis=0, keepdims=True)


def split(x):
    high = x.astype(jnp.bfloat16)
    low = (x - high.astype(jnp.float32)).astype(jnp.bfloat16)
    return high, low


def keep(pair_ref, x, rows=slice(None)):
    high, low = split(x)
    pair_ref[0, rows] = high
    pair_ref[1, rows] = low


def mm3(pair_ref, b, rows=slice(None)):
    high, low = b
    n = high.shape[1]
    wide = jnp.dot(
        pair_ref[0, rows], jnp.concatenate([high, low], axis=1), preferred_element_type=jnp.float32
    )
    cross = jnp.dot(pair_ref[1, rows], high, preferred_element_type=jnp.float32)
    return wide[:, :n] + (wide[:, n:] + cross)


N_IN = 11


def kernel(n_group, n_sub, *refs):
    hbm = refs[:N_IN]
    out_ref = refs[N_IN]
    held = refs[N_IN + 1 : 2 * N_IN + 1]
    (
        dense,
        dense_pair,
        near_pair,
        inv_diag,
        diag,
        basis_pair,
        basis_t_pair,
        select_pair,
        spread_pair,
        solve_pair,
        extend_out,
        extend_in,
        weight_out,
        weight_in,
        group_out,
        group_buf,
        sub_buf,
        face_out,
        face_in,
        group_dots,
        sub_dots,
        load_sem,
        send_sem,
        recv_sem,
        step_sem,
    ) = refs[2 * N_IN + 1 :]
    (
        rs_ref,
        mass_ref,
        values_ref,
        cols_ref,
        faces_ref,
        lands_ref,
        counts_ref,
        fweight_ref,
        factor_ref,
        basis_ref,
        coarse_ref,
    ) = held

    def load(i):
        return pltpu.make_async_copy(hbm[i], held[i], load_sem.at[i])

    for i in (9, 0, 4, 5, 6, 7, 10, 2, 3, 8, 1):
        load(i).start()

    me_g = lax.axis_index("group")
    me_s = lax.axis_index("sub")
    core = lax.rem(me_g, 2)
    sibling = me_g + 1 - 2 * core
    n_rows, n_rhs = rs_ref.shape
    n_slots = faces_ref.shape[1]
    per_peer = n_slots // n_sub
    n_blocks, n_stored = cols_ref.shape
    block_rows = n_rows // n_blocks
    n_coarse = basis_ref.shape[0]
    half = n_coarse // 2
    total_coarse = coarse_ref.shape[1]
    factor_rows = factor_ref.shape[1]
    n_factors = n_rows // factor_rows

    barrier = pltpu.get_barrier_semaphore()
    for step in range(1, n_group):
        peer = lax.rem(me_g + step, n_group)
        pl.semaphore_signal(barrier, inc=1, device_id=(peer, me_s), device_id_type=MESH)
    for step in range(1, n_sub):
        peer = lax.rem(me_s + step, n_sub)
        pl.semaphore_signal(barrier, inc=1, device_id=(me_g, peer), device_id_type=MESH)

    sent = []

    def send(src, dst, channel, arrived, peer):
        pltpu.make_async_remote_copy(
            src_ref=src,
            dst_ref=dst,
            send_sem=send_sem.at[channel],
            recv_sem=arrived,
            device_id=peer,
            device_id_type=MESH,
        ).start()

    def over_sub(channel, src_of, dst, arrived_of=None):
        for step in range(1, n_sub):
            peer = lax.rem(me_s + step, n_sub)
            arrived = recv_sem.at[channel] if arrived_of is None else arrived_of(step)
            send(src_of(peer), dst, channel, arrived, (me_g, peer))

    def over_group(channel, src_of, dst):
        for step in range(1, n_group):
            peer = lax.rem(me_g + step, n_group)
            send(src_of(peer), dst, channel, recv_sem.at[channel], (peer, me_s))

    def arrive(channel, part):
        pltpu.make_async_copy(part, part, recv_sem.at[channel]).wait()
        sent.append((channel, part))

    def message(phase):
        return pl.ds(0, half if phase == 0 else half + SUBLANES)

    def send_coarse(phase, part, dots):
        group_out[phase, 0] = jnp.concatenate([part[:half], dots], axis=0)
        group_out[phase, 1] = jnp.concatenate([part[half:], dots], axis=0)
        group_buf[phase, me_g] = group_out[phase, core]
        if phase == 0:
            pl.semaphore_wait(barrier, n_group - 1 + n_sub - 1)
        over_group(
            2 + phase,
            lambda peer: group_out.at[phase, lax.rem(peer, 2), message(phase)],
            group_buf.at[phase, me_g, message(phase)],
        )

    load(9).wait()
    load(0).wait()
    resid = rs_ref[...]
    send_coarse(0, mm(basis_ref[...], resid), jnp.zeros((SUBLANES, n_rhs), jnp.float32))

    for i in (4, 5, 6, 7):
        load(i).wait()
    slot = lax.broadcasted_iota(jnp.int32, (1, n_slots), 1)
    slot_peer = lax.broadcasted_iota(jnp.int32, (n_sub, n_slots), 1) // per_peer
    peer_ids = lax.broadcasted_iota(jnp.int32, (n_sub, n_slots), 0)
    of_peer = jnp.where(slot_peer == peer_ids, jnp.float32(1.0), jnp.float32(0.0))
    count_row = mm(
        jnp.broadcast_to(counts_ref[...].astype(jnp.float32), (SUBLANES, n_sub)), of_peer
    )[0:1]
    in_peer = (slot % per_peer).astype(jnp.float32)
    weights = jnp.where(in_peer < count_row - 0.5, fweight_ref[...], jnp.float32(0.0))
    row_ids = lax.broadcasted_iota(jnp.int32, (n_rows, n_slots), 0)
    face_hot = jnp.where(row_ids == faces_ref[...], weights, jnp.float32(0.0))
    land_hot = jnp.where(row_ids == lands_ref[...], jnp.float32(1.0), jnp.float32(0.0))
    spread = jnp.concatenate([land_hot, face_hot], axis=1)
    keep(spread_pair, spread)
    select = jnp.concatenate([face_hot, land_hot], axis=1).T
    keep(select_pair, select)

    weight_out[...] = mm(
        select[:n_slots, :], jnp.ones((n_rows, n_rhs), jnp.float32)
    ).reshape(n_sub, per_peer, n_rhs)
    weight_in[pl.ds(me_s, 1)] = weight_out[pl.ds(me_s, 1)]
    over_sub(0, lambda peer: weight_out.at[peer], weight_in.at[me_s])

    def gather_group(phase):
        arrive(2 + phase, group_buf.at[phase, pl.ds(0, n_group - 1), message(phase)])
        total = group_buf[phase, 0, message(phase)]
        for g in range(1, n_group):
            total = total + group_buf[phase, g, message(phase)]
        sub_buf[phase, core, me_s, message(phase)] = total
        mine = sub_buf.at[phase, core, me_s, message(phase)]
        over_sub(6 + phase, lambda peer: mine, mine, lambda step: step_sem.at[phase, step])
        forward(phase, me_s)

    def forward(phase, slot_of):
        part = sub_buf.at[phase, core, slot_of, pl.ds(0, half)]
        send(part, part, 13 + phase, recv_sem.at[13 + phase], (sibling, me_s))

    gather_group(0)

    load(10).wait()
    basis_t = basis_ref[...].T
    keep(basis_t_pair, basis_t)
    keep(basis_pair, basis_ref[...])
    keep(solve_pair, coarse_ref[...], slice(0, n_coarse))
    load(8).wait()
    for i in range(n_factors):
        rows = slice(i * factor_rows, (i + 1) * factor_rows)
        part = factor_ref[rows, :]
        keep(near_pair, mm(part.T, part), rows)

    load(2).wait()
    load(3).wait()
    n_tiles = n_rows // LANES
    stored = n_stored * block_rows
    stored_tiles = stored // LANES
    stored_ids = lax.broadcasted_iota(jnp.int32, (n_stored, stored), 0)
    lane_block = lax.broadcasted_iota(jnp.int32, (n_stored, stored), 1) // block_rows
    of_stored = jnp.where(stored_ids == lane_block, jnp.float32(1.0), jnp.float32(0.0))
    wide_cols = mm(cols_ref[...].astype(jnp.float32), of_stored)
    high = lax.broadcasted_iota(jnp.int32, (1, LANES), 1) // block_rows
    row_sums = mm(values_ref[...], jnp.ones((n_stored * block_rows, n_rhs), jnp.float32))
    col_parts = jnp.concatenate(
        [
            jnp.sum(values_ref[b * block_rows : (b + 1) * block_rows, :], axis=0, keepdims=True)
            for b in range(n_blocks)
        ],
        axis=0,
    )
    col_sums = [jnp.zeros((n_blocks, LANES), jnp.float32) for _ in range(n_tiles)]
    for t in range(stored_tiles):
        tile = col_parts[:, t * LANES : (t + 1) * LANES]
        turned = pltpu.roll(tile, block_rows, 1)
        straight_cols = wide_cols[:, t * LANES : (t + 1) * LANES]
        turned_cols = pltpu.roll(straight_cols, block_rows, 1)
        for u in range(n_tiles):
            target = (2 * u + high).astype(jnp.float32)
            col_sums[u] = (
                col_sums[u]
                + jnp.where(jnp.abs(straight_cols - target) < 0.5, tile, jnp.float32(0.0))
                + jnp.where(jnp.abs(turned_cols - target) < 0.5, turned, jnp.float32(0.0))
            )
    col_row = jnp.concatenate(
        [jnp.sum(part, axis=0, keepdims=True) for part in col_sums], axis=1
    )
    load(1).wait()
    mass_col = jnp.broadcast_to(mass_ref[...] + col_row, (n_rhs, n_rows)).T
    arrive(0, weight_in.at[pl.ds(0, n_sub - 1)])
    degree = row_sums + mm(
        spread,
        jnp.concatenate(
            [
                weight_in[...].reshape(n_slots, n_rhs),
                jnp.ones((n_slots, n_rhs), jnp.float32),
            ],
            axis=0,
        ),
    )
    diag[...] = mass_col + degree
    inv_diag[...] = 1.0 / diag[...]

    def local_of(field, pair):
        parts = []
        for i in range(n_factors):
            rows = slice(i * factor_rows, (i + 1) * factor_rows)
            parts.append(mm3(near_pair, (pair[0][rows], pair[1][rows]), rows))
        return field * inv_diag[...] + jnp.concatenate(parts, axis=0)

    def send_faces(phase, field):
        picked = mm3(select_pair, split(field))
        face_out[phase, :, :per_peer, :] = picked[:n_slots].reshape(n_sub, per_peer, n_rhs)
        face_out[phase, :, per_peer:, :] = picked[n_slots:].reshape(n_sub, per_peer, n_rhs)
        face_in[phase, me_s] = face_out[phase, me_s]
        over_sub(10 + phase, lambda peer: face_out.at[phase, peer], face_in.at[phase, me_s])

    def receive(phase, local_part):
        for step in range(1, n_sub):
            origin = lax.rem(me_s + n_sub - step, n_sub)
            part = sub_buf.at[phase, core, origin, message(phase)]
            pltpu.make_async_copy(part, part, step_sem.at[phase, step]).wait()
            forward(phase, origin)
        dots = None if phase == 0 else jnp.sum(sub_buf[phase, core, :, half:, :], axis=0)
        if phase == 1:
            arrive(1, extend_in.at[pl.ds(0, n_sub - 1)])
            keep(
                solve_pair,
                extend_in[...].reshape(2 * n_slots, total_coarse),
                slice(n_coarse, n_coarse + 2 * n_slots),
            )
        sent.append((6 + phase, sub_buf.at[phase, 0, pl.ds(0, n_sub - 1), message(phase)]))
        arrive(13 + phase, sub_buf.at[phase, 0, :, pl.ds(0, half)])
        whole = jnp.concatenate(
            [sub_buf[phase, 0, :, :half, :], sub_buf[phase, 1, :, :half, :]], axis=1
        ).reshape(total_coarse, n_rhs)
        pair = split(whole)
        if phase == 0:
            solved = mm3(solve_pair, pair, slice(0, n_coarse))
            return local_part + mm3(basis_t_pair, split(solved)), None, None
        solved = mm3(solve_pair, pair)
        field = local_part + mm3(basis_t_pair, split(solved[:n_coarse]))
        return field, receive_faces(phase, solved[n_coarse:]), dots

    def receive_faces(phase, solved):
        arrive(10 + phase, face_in.at[phase, pl.ds(0, n_sub - 1)])
        far = face_in[phase]
        if solved is not None:
            far = far + solved.reshape(n_sub, 2 * per_peer, n_rhs)
        return jnp.concatenate(
            [
                far[:, :per_peer, :].reshape(n_slots, n_rhs),
                far[:, per_peer:, :].reshape(n_slots, n_rhs),
            ],
            axis=0,
        )

    def operate(field, far):
        pair = split(field)
        held_field = pair[0].astype(jnp.float32) + pair[1].astype(jnp.float32)
        return diag[...] * held_field - mm3(dense_pair, pair) - mm3(spread_pair, split(far))

    z, _, _ = receive(0, local_of(resid, split(resid)))
    send_faces(0, z)
    reach = mm(mm(select, basis_t), coarse_ref[...])
    extend_out[:, :per_peer, :] = reach[:n_slots].reshape(n_sub, per_peer, total_coarse)
    extend_out[:, per_peer:, :] = reach[n_slots:].reshape(n_sub, per_peer, total_coarse)
    extend_in[pl.ds(me_s, 1)] = extend_out[pl.ds(me_s, 1)]
    over_sub(1, lambda peer: extend_out.at[peer], extend_in.at[me_s])

    for b in range(n_blocks):
        rows = slice(b * block_rows, (b + 1) * block_rows)
        sums = [jnp.zeros((block_rows, LANES), jnp.float32) for _ in range(n_tiles)]
        for t in range(stored_tiles):
            tile = values_ref[rows, t * LANES : (t + 1) * LANES]
            turned = pltpu.roll(tile, block_rows, 1)
            straight_cols = wide_cols[b : b + 1, t * LANES : (t + 1) * LANES]
            turned_cols = pltpu.roll(straight_cols, block_rows, 1)
            for u in range(n_tiles):
                target = (2 * u + high).astype(jnp.float32)
                straight = jnp.abs(straight_cols - target) < 0.5
                swapped = jnp.abs(turned_cols - target) < 0.5
                sums[u] = (
                    sums[u]
                    + jnp.where(straight, tile, jnp.float32(0.0))
                    + jnp.where(swapped, turned, jnp.float32(0.0))
                )
        for u in range(n_tiles):
            dense[rows, u * LANES : (u + 1) * LANES] = sums[u]
    keep(dense_pair, dense[...] + dense[...].T)
    z_far = receive_faces(0, None)
    image = operate(z, z_far)
    pair = split(image)
    send_coarse(
        1, mm3(basis_pair, pair), stack_dots([column_dot(resid, z), column_dot(z, image)])
    )
    local_part = local_of(image, pair)
    send_faces(1, local_part)
    gather_group(1)
    m_image, m_far, dots = receive(1, local_part)
    gamma, bent = dots[0:1], dots[1:2]
    alpha = gamma / bent
    direction = z
    answer = alpha * direction
    resid = resid - alpha * image
    z = z - alpha * m_image
    z_far = z_far - alpha * m_far
    z_image = operate(z, z_far)
    pair = split(z_image)
    send_coarse(
        2,
        mm3(basis_pair, pair),
        stack_dots([column_dot(resid, z), column_dot(z, z_image), column_dot(z, image)]),
    )
    local_part = local_of(z_image, pair)
    send_faces(2, local_part)
    gather_group(2)
    m_z_image, m_z_far, dots = receive(2, local_part)
    beta = dots[0:1] / gamma
    gamma = dots[0:1]
    bent = dots[1:2] + beta * (2.0 * dots[2:3] + beta * bent)
    alpha = gamma / bent
    direction = z + beta * direction
    image = z_image + beta * image
    answer = answer + alpha * direction
    resid = resid - alpha * image
    z = z - alpha * (m_z_image + beta * m_image)
    z_far = z_far - alpha * (m_z_far + beta * m_far)
    z_image = operate(z, z_far)
    group_dots[me_g] = stack_dots(
        [column_dot(resid, z), column_dot(z, z_image), column_dot(z, image)]
    )
    over_group(5, lambda peer: group_dots.at[me_g], group_dots.at[me_g])
    arrive(5, group_dots.at[pl.ds(0, n_group - 1)])
    sub_dots[me_s] = jnp.sum(group_dots[...], axis=0)
    over_sub(9, lambda peer: sub_dots.at[me_s], sub_dots.at[me_s])
    arrive(9, sub_dots.at[pl.ds(0, n_sub - 1)])
    dots = jnp.sum(sub_dots[...], axis=0)
    beta = dots[0:1] / gamma
    gamma = dots[0:1]
    bent = dots[1:2] + beta * (2.0 * dots[2:3] + beta * bent)
    alpha = gamma / bent
    out_ref[0] = answer + alpha * (z + beta * direction)
    out_ref[1] = resid - alpha * (z_image + beta * image)

    for channel, part in sent:
        pltpu.make_async_copy(part, part, send_sem.at[channel]).wait()


def local(n_group, n_sub, *args):
    right_side, face_rows = args[0], args[4]
    basis, coarse_inverse = args[9], args[10]
    n_rows, n_rhs = right_side.shape
    n_slots = face_rows.shape[1]
    per_peer = n_slots // n_sub
    n_coarse = basis.shape[0]
    total_coarse = coarse_inverse.shape[1]
    factor_rows = args[8].shape[1]
    f32 = jnp.float32
    bf16 = jnp.bfloat16
    vmem = pl.BlockSpec(memory_space=pltpu.VMEM)
    message = n_coarse // 2 + SUBLANES
    scratch = [pltpu.VMEM(arg.shape, arg.dtype) for arg in args]
    scratch += [
        pltpu.VMEM((n_rows, n_rows), f32),
        pltpu.VMEM((2, n_rows, n_rows), bf16),
        pltpu.VMEM((2, n_rows, factor_rows), bf16),
        pltpu.VMEM((n_rows, n_rhs), f32),
        pltpu.VMEM((n_rows, n_rhs), f32),
        pltpu.VMEM((2, n_coarse, n_rows), bf16),
        pltpu.VMEM((2, n_rows, n_coarse), bf16),
        pltpu.VMEM((2, 2 * n_slots, n_rows), bf16),
        pltpu.VMEM((2, n_rows, 2 * n_slots), bf16),
        pltpu.VMEM((2, n_coarse + 2 * n_slots, total_coarse), bf16),
        pltpu.VMEM((n_sub, 2 * per_peer, total_coarse), f32),
        pltpu.VMEM((n_sub, 2 * per_peer, total_coarse), f32),
        pltpu.VMEM((n_sub, per_peer, n_rhs), f32),
        pltpu.VMEM((n_sub, per_peer, n_rhs), f32),
        pltpu.VMEM((3, 2, message, n_rhs), f32),
        pltpu.VMEM((3, n_group, message, n_rhs), f32),
        pltpu.VMEM((3, 2, n_sub, message, n_rhs), f32),
        pltpu.VMEM((3, n_sub, 2 * per_peer, n_rhs), f32),
        pltpu.VMEM((3, n_sub, 2 * per_peer, n_rhs), f32),
        pltpu.VMEM((n_group, SUBLANES, n_rhs), f32),
        pltpu.VMEM((n_sub, SUBLANES, n_rhs), f32),
        pltpu.SemaphoreType.DMA((N_IN,)),
        pltpu.SemaphoreType.DMA((16,)),
        pltpu.SemaphoreType.DMA((16,)),
        pltpu.SemaphoreType.DMA((3, n_sub)),
    ]
    field = jax.ShapeDtypeStruct((2, n_rows, n_rhs), f32)
    both = pl.pallas_call(
        functools.partial(kernel, n_group, n_sub),
        out_shape=field,
        in_specs=[pl.BlockSpec(memory_space=pl.ANY)] * N_IN,
        out_specs=vmem,
        scratch_shapes=scratch,
        compiler_params=pltpu.CompilerParams(
            collective_id=0, has_side_effects=True, vmem_limit_bytes=56 * 1024 * 1024
        ),
    )(*args)
    return both[0], both[1]


def solution(mesh):
    n_group, n_sub = mesh.shape["group"], mesh.shape["sub"]
    rows = P(("group", "sub"), None)
    return jax.shard_map(
        functools.partial(local, n_group, n_sub),
        mesh=mesh,
        in_specs=(rows,) * 10 + (P("sub", None),),
        out_specs=(rows, rows),
        check_vma=False,
    )
```

```python
import functools

import jax
import jax.numpy as jnp
from jax import lax
from jax.experimental import pallas as pl
from jax.experimental.pallas import tpu as pltpu
from jax.sharding import PartitionSpec as P

HIGHEST = lax.Precision.HIGHEST
MESH = pl.DeviceIdType.MESH
LANES = 128
SUBLANES = 8
DOTS = 4


def mm(a, b):
    return jnp.dot(a, b, precision=HIGHEST, preferred_element_type=jnp.float32)


def stack_dots(rows):
    pad = SUBLANES - len(rows)
    return jnp.concatenate(rows + [jnp.zeros((pad, rows[0].shape[1]), jnp.float32)], axis=0)


def column_dot(a, b):
    return jnp.sum(a * b, axis=0, keepdims=True)


def split(x):
    high = x.astype(jnp.bfloat16)
    low = (x - high.astype(jnp.float32)).astype(jnp.bfloat16)
    return high, low


def keep(pair_ref, x, rows=slice(None)):
    high, low = split(x)
    pair_ref[0, rows] = high
    pair_ref[1, rows] = low


def mm3(pair_ref, b, rows=slice(None)):
    high, low = b
    n = high.shape[1]
    wide = jnp.dot(
        pair_ref[0, rows], jnp.concatenate([high, low], axis=1), preferred_element_type=jnp.float32
    )
    cross = jnp.dot(pair_ref[1, rows], high, preferred_element_type=jnp.float32)
    return wide[:, :n] + (wide[:, n:] + cross)


N_IN = 11


def kernel(n_group, n_sub, *refs):
    hbm = refs[:N_IN]
    out_ref = refs[N_IN]
    held = refs[N_IN + 1 : 2 * N_IN + 1]
    (
        dense,
        dense_pair,
        near_pair,
        inv_diag,
        diag,
        basis_pair,
        basis_t_pair,
        select_pair,
        spread_pair,
        solve_pair,
        extend_out,
        extend_in,
        weight_out,
        weight_in,
        group_out,
        group_buf,
        sub_buf,
        face_out,
        face_in,
        group_dots,
        sub_dots,
        load_sem,
        send_sem,
        recv_sem,
        step_sem,
    ) = refs[2 * N_IN + 1 :]
    (
        rs_ref,
        mass_ref,
        values_ref,
        cols_ref,
        faces_ref,
        lands_ref,
        counts_ref,
        fweight_ref,
        factor_ref,
        basis_ref,
        coarse_ref,
    ) = held

    def load(i):
        return pltpu.make_async_copy(hbm[i], held[i], load_sem.at[i])

    for i in (9, 0, 4, 5, 6, 7, 10, 2, 3, 8, 1):
        load(i).start()

    me_g = lax.axis_index("group")
    me_s = lax.axis_index("sub")
    core = lax.rem(me_g, 2)
    sibling = me_g + 1 - 2 * core
    n_rows, n_rhs = rs_ref.shape
    n_slots = faces_ref.shape[1]
    per_peer = n_slots // n_sub
    n_blocks, n_stored = cols_ref.shape
    block_rows = n_rows // n_blocks
    n_coarse = basis_ref.shape[0]
    half = n_coarse // 2
    total_coarse = coarse_ref.shape[1]
    factor_rows = factor_ref.shape[1]
    n_factors = n_rows // factor_rows

    barrier = pltpu.get_barrier_semaphore()
    for step in range(1, n_group):
        peer = lax.rem(me_g + step, n_group)
        pl.semaphore_signal(barrier, inc=1, device_id=(peer, me_s), device_id_type=MESH)
    for step in range(1, n_sub):
        peer = lax.rem(me_s + step, n_sub)
        pl.semaphore_signal(barrier, inc=1, device_id=(me_g, peer), device_id_type=MESH)

    sent = []

    def send(src, dst, channel, arrived, peer):
        pltpu.make_async_remote_copy(
            src_ref=src,
            dst_ref=dst,
            send_sem=send_sem.at[channel],
            recv_sem=arrived,
            device_id=peer,
            device_id_type=MESH,
        ).start()

    def over_sub(channel, src_of, dst, arrived_of=None):
        for step in range(1, n_sub):
            peer = lax.rem(me_s + step, n_sub)
            arrived = recv_sem.at[channel] if arrived_of is None else arrived_of(step)
            send(src_of(peer), dst, channel, arrived, (me_g, peer))

    def over_group(channel, src_of, dst):
        for step in range(1, n_group):
            peer = lax.rem(me_g + step, n_group)
            send(src_of(peer), dst, channel, recv_sem.at[channel], (peer, me_s))

    def arrive(channel, part):
        pltpu.make_async_copy(part, part, recv_sem.at[channel]).wait()
        sent.append((channel, part))

    def message(phase):
        return pl.ds(0, half if phase == 0 else half + DOTS)

    def send_coarse(phase, part, dots):
        group_out[phase, 0] = jnp.concatenate([part[:half], dots], axis=0)
        group_out[phase, 1] = jnp.concatenate([part[half:], dots], axis=0)
        group_buf[phase, me_g] = group_out[phase, core]
        if phase == 0:
            pl.semaphore_wait(barrier, n_group - 1 + n_sub - 1)
        over_group(
            2 + phase,
            lambda peer: group_out.at[phase, lax.rem(peer, 2), message(phase)],
            group_buf.at[phase, me_g, message(phase)],
        )

    load(9).wait()
    load(0).wait()
    resid = rs_ref[...]
    send_coarse(0, mm(basis_ref[...], resid), jnp.zeros((SUBLANES, n_rhs), jnp.float32))

    for i in (4, 5, 6, 7):
        load(i).wait()
    slot = lax.broadcasted_iota(jnp.int32, (1, n_slots), 1)
    slot_peer = lax.broadcasted_iota(jnp.int32, (n_sub, n_slots), 1) // per_peer
    peer_ids = lax.broadcasted_iota(jnp.int32, (n_sub, n_slots), 0)
    of_peer = jnp.where(slot_peer == peer_ids, jnp.float32(1.0), jnp.float32(0.0))
    count_row = mm(
        jnp.broadcast_to(counts_ref[...].astype(jnp.float32), (SUBLANES, n_sub)), of_peer
    )[0:1]
    in_peer = (slot % per_peer).astype(jnp.float32)
    weights = jnp.where(in_peer < count_row - 0.5, fweight_ref[...], jnp.float32(0.0))
    row_ids = lax.broadcasted_iota(jnp.int32, (n_rows, n_slots), 0)
    face_hot = jnp.where(row_ids == faces_ref[...], weights, jnp.float32(0.0))
    land_hot = jnp.where(row_ids == lands_ref[...], jnp.float32(1.0), jnp.float32(0.0))
    spread = jnp.concatenate([land_hot, face_hot], axis=1)
    keep(spread_pair, spread)
    select = jnp.concatenate([face_hot, land_hot], axis=1).T
    keep(select_pair, select)

    weight_out[...] = mm(
        select[:n_slots, :], jnp.ones((n_rows, n_rhs), jnp.float32)
    ).reshape(n_sub, per_peer, n_rhs)
    weight_in[pl.ds(me_s, 1)] = weight_out[pl.ds(me_s, 1)]
    over_sub(0, lambda peer: weight_out.at[peer], weight_in.at[me_s])

    def gather_group(phase):
        arrive(2 + phase, group_buf.at[phase, pl.ds(0, n_group - 1), message(phase)])
        total = group_buf[phase, 0, message(phase)]
        for g in range(1, n_group):
            total = total + group_buf[phase, g, message(phase)]
        sub_buf[phase, core, me_s, message(phase)] = total
        mine = sub_buf.at[phase, core, me_s, message(phase)]
        over_sub(6 + phase, lambda peer: mine, mine, lambda step: step_sem.at[phase, step])
        forward(phase, me_s)

    def forward(phase, slot_of):
        part = sub_buf.at[phase, core, slot_of, pl.ds(0, half)]
        send(part, part, 13 + phase, recv_sem.at[13 + phase], (sibling, me_s))

    def keep_solve(rows_of, rows):
        for part in range(2):
            columns = slice(part * (total_coarse // 2), (part + 1) * (total_coarse // 2))
            keep(solve_pair.at[part], rows_of[:, columns], rows)

    gather_group(0)

    load(10).wait()
    basis_t = basis_ref[...].T
    keep(basis_t_pair, basis_t)
    keep(basis_pair, basis_ref[...])
    by_row = coarse_ref[...].T.reshape(n_sub, n_coarse, n_coarse)
    coarse = jnp.concatenate(
        [
            by_row[:, :half].reshape(total_coarse // 2, n_coarse),
            by_row[:, half:].reshape(total_coarse // 2, n_coarse),
        ],
        axis=0,
    ).T
    keep_solve(coarse, slice(0, n_coarse))
    load(8).wait()
    for i in range(n_factors):
        rows = slice(i * factor_rows, (i + 1) * factor_rows)
        part = factor_ref[rows, :]
        keep(near_pair, mm(part.T, part), rows)

    load(2).wait()
    load(3).wait()
    n_tiles = n_rows // LANES
    stored = n_stored * block_rows
    stored_tiles = stored // LANES
    stored_ids = lax.broadcasted_iota(jnp.int32, (n_stored, stored), 0)
    lane_block = lax.broadcasted_iota(jnp.int32, (n_stored, stored), 1) // block_rows
    of_stored = jnp.where(stored_ids == lane_block, jnp.float32(1.0), jnp.float32(0.0))
    wide_cols = mm(cols_ref[...].astype(jnp.float32), of_stored)
    high = lax.broadcasted_iota(jnp.int32, (1, LANES), 1) // block_rows
    row_sums = mm(values_ref[...], jnp.ones((n_stored * block_rows, n_rhs), jnp.float32))
    col_parts = jnp.concatenate(
        [
            jnp.sum(values_ref[b * block_rows : (b + 1) * block_rows, :], axis=0, keepdims=True)
            for b in range(n_blocks)
        ],
        axis=0,
    )
    col_sums = [jnp.zeros((n_blocks, LANES), jnp.float32) for _ in range(n_tiles)]
    for t in range(stored_tiles):
        tile = col_parts[:, t * LANES : (t + 1) * LANES]
        turned = pltpu.roll(tile, block_rows, 1)
        straight_cols = wide_cols[:, t * LANES : (t + 1) * LANES]
        turned_cols = pltpu.roll(straight_cols, block_rows, 1)
        for u in range(n_tiles):
            target = (2 * u + high).astype(jnp.float32)
            col_sums[u] = (
                col_sums[u]
                + jnp.where(jnp.abs(straight_cols - target) < 0.5, tile, jnp.float32(0.0))
                + jnp.where(jnp.abs(turned_cols - target) < 0.5, turned, jnp.float32(0.0))
            )
    col_row = jnp.concatenate(
        [jnp.sum(part, axis=0, keepdims=True) for part in col_sums], axis=1
    )
    load(1).wait()
    mass_col = jnp.broadcast_to(mass_ref[...] + col_row, (n_rhs, n_rows)).T
    arrive(0, weight_in.at[pl.ds(0, n_sub - 1)])
    degree = row_sums + mm(
        spread,
        jnp.concatenate(
            [
                weight_in[...].reshape(n_slots, n_rhs),
                jnp.ones((n_slots, n_rhs), jnp.float32),
            ],
            axis=0,
        ),
    )
    diag[...] = mass_col + degree
    inv_diag[...] = 1.0 / diag[...]

    def local_of(field, pair):
        parts = []
        for i in range(n_factors):
            rows = slice(i * factor_rows, (i + 1) * factor_rows)
            parts.append(mm3(near_pair, (pair[0][rows], pair[1][rows]), rows))
        return field * inv_diag[...] + jnp.concatenate(parts, axis=0)

    def send_faces(phase, field):
        picked = mm3(select_pair, split(field))
        face_out[phase, :, :per_peer, :] = picked[:n_slots].reshape(n_sub, per_peer, n_rhs)
        face_out[phase, :, per_peer:, :] = picked[n_slots:].reshape(n_sub, per_peer, n_rhs)
        face_in[phase, me_s] = face_out[phase, me_s]
        over_sub(10 + phase, lambda peer: face_out.at[phase, peer], face_in.at[phase, me_s])

    def receive(phase, local_part):
        if phase == 1:
            arrive(1, extend_in.at[pl.ds(0, n_sub - 1)])
            keep_solve(
                extend_in[...].reshape(2 * n_slots, total_coarse),
                slice(n_coarse, n_coarse + 2 * n_slots),
            )
        for step in range(1, n_sub):
            origin = lax.rem(me_s + n_sub - step, n_sub)
            part = sub_buf.at[phase, core, origin, message(phase)]
            pltpu.make_async_copy(part, part, step_sem.at[phase, step]).wait()
            forward(phase, origin)
        dots = None if phase == 0 else jnp.sum(sub_buf[phase, core, :, half : half + DOTS, :], axis=0)
        sent.append((6 + phase, sub_buf.at[phase, 0, pl.ds(0, n_sub - 1), message(phase)]))
        rows = slice(0, n_coarse if phase == 0 else n_coarse + 2 * n_slots)

        def solve_half(part):
            gathered = sub_buf[phase, part, :, :half, :].reshape(total_coarse // 2, n_rhs)
            return mm3(solve_pair.at[part], split(gathered), rows)

        solved = solve_half(core)
        arrive(13 + phase, sub_buf.at[phase, 0, :, pl.ds(0, half)])
        solved = solved + solve_half(1 - core)
        if phase == 0:
            return local_part + mm3(basis_t_pair, split(solved)), None, None
        field = local_part + mm3(basis_t_pair, split(solved[:n_coarse]))
        return field, receive_faces(phase, solved[n_coarse:]), dots

    def receive_faces(phase, solved):
        arrive(10 + phase, face_in.at[phase, pl.ds(0, n_sub - 1)])
        far = face_in[phase]
        if solved is not None:
            far = far + solved.reshape(n_sub, 2 * per_peer, n_rhs)
        return jnp.concatenate(
            [
                far[:, :per_peer, :].reshape(n_slots, n_rhs),
                far[:, per_peer:, :].reshape(n_slots, n_rhs),
            ],
            axis=0,
        )

    def operate(field, far):
        pair = split(field)
        held_field = pair[0].astype(jnp.float32) + pair[1].astype(jnp.float32)
        return diag[...] * held_field - mm3(dense_pair, pair) - mm3(spread_pair, split(far))

    z, _, _ = receive(0, local_of(resid, split(resid)))
    send_faces(0, z)
    reach = mm(mm(select, basis_t), coarse)
    extend_out[:, :per_peer, :] = reach[:n_slots].reshape(n_sub, per_peer, total_coarse)
    extend_out[:, per_peer:, :] = reach[n_slots:].reshape(n_sub, per_peer, total_coarse)
    extend_in[pl.ds(me_s, 1)] = extend_out[pl.ds(me_s, 1)]
    over_sub(1, lambda peer: extend_out.at[peer], extend_in.at[me_s])

    for b in range(n_blocks):
        rows = slice(b * block_rows, (b + 1) * block_rows)
        sums = [jnp.zeros((block_rows, LANES), jnp.float32) for _ in range(n_tiles)]
        for t in range(stored_tiles):
            tile = values_ref[rows, t * LANES : (t + 1) * LANES]
            turned = pltpu.roll(tile, block_rows, 1)
            straight_cols = wide_cols[b : b + 1, t * LANES : (t + 1) * LANES]
            turned_cols = pltpu.roll(straight_cols, block_rows, 1)
            for u in range(n_tiles):
                target = (2 * u + high).astype(jnp.float32)
                straight = jnp.abs(straight_cols - target) < 0.5
                swapped = jnp.abs(turned_cols - target) < 0.5
                sums[u] = (
                    sums[u]
                    + jnp.where(straight, tile, jnp.float32(0.0))
                    + jnp.where(swapped, turned, jnp.float32(0.0))
                )
        for u in range(n_tiles):
            dense[rows, u * LANES : (u + 1) * LANES] = sums[u]
    keep(dense_pair, dense[...] + dense[...].T)
    z_far = receive_faces(0, None)
    image = operate(z, z_far)
    pair = split(image)
    send_coarse(
        1, mm3(basis_pair, pair), stack_dots([column_dot(resid, z), column_dot(z, image)])
    )
    local_part = local_of(image, pair)
    send_faces(1, local_part)
    gather_group(1)
    m_image, m_far, dots = receive(1, local_part)
    gamma, bent = dots[0:1], dots[1:2]
    alpha = gamma / bent
    direction = z
    first_alpha = alpha
    resid = resid - alpha * image
    z = z - alpha * m_image
    z_far = z_far - alpha * m_far
    z_image = operate(z, z_far)
    pair = split(z_image)
    send_coarse(
        2,
        mm3(basis_pair, pair),
        stack_dots([column_dot(resid, z), column_dot(z, z_image), column_dot(z, image)]),
    )
    local_part = local_of(z_image, pair)
    send_faces(2, local_part)
    gather_group(2)
    answer = first_alpha * direction
    m_z_image, m_z_far, dots = receive(2, local_part)
    beta = dots[0:1] / gamma
    gamma = dots[0:1]
    bent = dots[1:2] + beta * (2.0 * dots[2:3] + beta * bent)
    alpha = gamma / bent
    last_z, last_beta, last_alpha = z, beta, alpha
    z_far = z_far - alpha * (m_z_far + beta * m_far)
    z = z - alpha * (m_z_image + beta * m_image)
    image = z_image + beta * image
    resid = resid - alpha * image
    z_image = operate(z, z_far)
    group_dots[me_g] = stack_dots(
        [column_dot(resid, z), column_dot(z, z_image), column_dot(z, image)]
    )
    over_group(5, lambda peer: group_dots.at[me_g], group_dots.at[me_g])
    direction = last_z + last_beta * direction
    answer = answer + last_alpha * direction
    arrive(5, group_dots.at[pl.ds(0, n_group - 1)])
    sub_dots[me_s] = jnp.sum(group_dots[...], axis=0)
    over_sub(9, lambda peer: sub_dots.at[me_s], sub_dots.at[me_s])
    arrive(9, sub_dots.at[pl.ds(0, n_sub - 1)])
    dots = jnp.sum(sub_dots[...], axis=0)
    beta = dots[0:1] / gamma
    gamma = dots[0:1]
    bent = dots[1:2] + beta * (2.0 * dots[2:3] + beta * bent)
    alpha = gamma / bent
    out_ref[0] = answer + alpha * (z + beta * direction)
    out_ref[1] = resid - alpha * (z_image + beta * image)

    for channel, part in sent:
        pltpu.make_async_copy(part, part, send_sem.at[channel]).wait()


def local(n_group, n_sub, *args):
    right_side, face_rows = args[0], args[4]
    basis, coarse_inverse = args[9], args[10]
    n_rows, n_rhs = right_side.shape
    n_slots = face_rows.shape[1]
    per_peer = n_slots // n_sub
    n_coarse = basis.shape[0]
    total_coarse = coarse_inverse.shape[1]
    factor_rows = args[8].shape[1]
    f32 = jnp.float32
    bf16 = jnp.bfloat16
    vmem = pl.BlockSpec(memory_space=pltpu.VMEM)
    message = n_coarse // 2 + SUBLANES
    scratch = [pltpu.VMEM(arg.shape, arg.dtype) for arg in args]
    scratch += [
        pltpu.VMEM((n_rows, n_rows), f32),
        pltpu.VMEM((2, n_rows, n_rows), bf16),
        pltpu.VMEM((2, n_rows, factor_rows), bf16),
        pltpu.VMEM((n_rows, n_rhs), f32),
        pltpu.VMEM((n_rows, n_rhs), f32),
        pltpu.VMEM((2, n_coarse, n_rows), bf16),
        pltpu.VMEM((2, n_rows, n_coarse), bf16),
        pltpu.VMEM((2, 2 * n_slots, n_rows), bf16),
        pltpu.VMEM((2, n_rows, 2 * n_slots), bf16),
        pltpu.VMEM((2, 2, n_coarse + 2 * n_slots, total_coarse // 2), bf16),
        pltpu.VMEM((n_sub, 2 * per_peer, total_coarse), f32),
        pltpu.VMEM((n_sub, 2 * per_peer, total_coarse), f32),
        pltpu.VMEM((n_sub, per_peer, n_rhs), f32),
        pltpu.VMEM((n_sub, per_peer, n_rhs), f32),
        pltpu.VMEM((3, 2, message, n_rhs), f32),
        pltpu.VMEM((3, n_group, message, n_rhs), f32),
        pltpu.VMEM((3, 2, n_sub, message, n_rhs), f32),
        pltpu.VMEM((3, n_sub, 2 * per_peer, n_rhs), f32),
        pltpu.VMEM((3, n_sub, 2 * per_peer, n_rhs), f32),
        pltpu.VMEM((n_group, SUBLANES, n_rhs), f32),
        pltpu.VMEM((n_sub, SUBLANES, n_rhs), f32),
        pltpu.SemaphoreType.DMA((N_IN,)),
        pltpu.SemaphoreType.DMA((16,)),
        pltpu.SemaphoreType.DMA((16,)),
        pltpu.SemaphoreType.DMA((3, n_sub)),
    ]
    field = jax.ShapeDtypeStruct((2, n_rows, n_rhs), f32)
    both = pl.pallas_call(
        functools.partial(kernel, n_group, n_sub),
        out_shape=field,
        in_specs=[pl.BlockSpec(memory_space=pl.ANY)] * N_IN,
        out_specs=vmem,
        scratch_shapes=scratch,
        compiler_params=pltpu.CompilerParams(
            collective_id=0, has_side_effects=True, vmem_limit_bytes=56 * 1024 * 1024
        ),
    )(*args)
    return both[0], both[1]


def solution(mesh):
    n_group, n_sub = mesh.shape["group"], mesh.shape["sub"]
    rows = P(("group", "sub"), None)
    return jax.shard_map(
        functools.partial(local, n_group, n_sub),
        mesh=mesh,
        in_specs=(rows,) * 10 + (P("sub", None),),
        out_specs=(rows, rows),
        check_vma=False,
    )
```

```python
import functools

import jax
import jax.numpy as jnp
from jax import lax
from jax.experimental import pallas as pl
from jax.experimental.pallas import tpu as pltpu
from jax.sharding import PartitionSpec as P

HIGHEST = lax.Precision.HIGHEST
MESH = pl.DeviceIdType.MESH
LANES = 128
SUBLANES = 8
DOTS = 4


def mm(a, b):
    return jnp.dot(a, b, precision=HIGHEST, preferred_element_type=jnp.float32)


def stack_dots(rows):
    pad = SUBLANES - len(rows)
    return jnp.concatenate(rows + [jnp.zeros((pad, rows[0].shape[1]), jnp.float32)], axis=0)


def column_dot(a, b):
    return jnp.sum(a * b, axis=0, keepdims=True)


def split(x):
    high = x.astype(jnp.bfloat16)
    low = (x - high.astype(jnp.float32)).astype(jnp.bfloat16)
    return high, low


def keep(pair_ref, x, rows=slice(None)):
    high, low = split(x)
    pair_ref[0, rows] = high
    pair_ref[1, rows] = low


def mm3(pair_ref, b, rows=slice(None)):
    high, low = b
    n = high.shape[1]
    wide = jnp.dot(
        pair_ref[0, rows], jnp.concatenate([high, low], axis=1), preferred_element_type=jnp.float32
    )
    cross = jnp.dot(pair_ref[1, rows], high, preferred_element_type=jnp.float32)
    return wide[:, :n] + (wide[:, n:] + cross)


N_IN = 11


def kernel(n_group, n_sub, *refs):
    hbm = refs[:N_IN]
    out_ref = refs[N_IN]
    held = refs[N_IN + 1 : 2 * N_IN + 1]
    (
        dense,
        dense_pair,
        near_pair,
        inv_diag,
        diag,
        basis_pair,
        basis_t_pair,
        select_pair,
        spread_pair,
        solve_pair,
        extend_out,
        extend_in,
        weight_out,
        weight_in,
        group_out,
        group_buf,
        sub_buf,
        face_out,
        face_in,
        group_dots,
        sub_dots,
        load_sem,
        send_sem,
        recv_sem,
        step_sem,
    ) = refs[2 * N_IN + 1 :]
    (
        rs_ref,
        mass_ref,
        values_ref,
        cols_ref,
        faces_ref,
        lands_ref,
        counts_ref,
        fweight_ref,
        factor_ref,
        basis_ref,
        coarse_ref,
    ) = held

    def load(i):
        return pltpu.make_async_copy(hbm[i], held[i], load_sem.at[i])

    for i in (9, 0, 4, 5, 6, 7, 10, 2, 3, 8, 1):
        load(i).start()

    me_g = lax.axis_index("group")
    me_s = lax.axis_index("sub")
    core = lax.rem(me_g, 2)
    sibling = me_g + 1 - 2 * core
    n_rows, n_rhs = rs_ref.shape
    n_slots = faces_ref.shape[1]
    per_peer = n_slots // n_sub
    n_blocks, n_stored = cols_ref.shape
    block_rows = n_rows // n_blocks
    n_coarse = basis_ref.shape[0]
    half = n_coarse // 2
    total_coarse = coarse_ref.shape[1]
    factor_rows = factor_ref.shape[1]
    n_factors = n_rows // factor_rows

    barrier = pltpu.get_barrier_semaphore()
    for step in range(1, n_group):
        peer = lax.rem(me_g + step, n_group)
        pl.semaphore_signal(barrier, inc=1, device_id=(peer, me_s), device_id_type=MESH)
    for step in range(1, n_sub):
        peer = lax.rem(me_s + step, n_sub)
        pl.semaphore_signal(barrier, inc=1, device_id=(me_g, peer), device_id_type=MESH)

    sent = []
    far_first = sorted(range(1, n_sub), key=lambda step: abs(step - n_sub // 2))

    def send(src, dst, channel, arrived, peer):
        pltpu.make_async_remote_copy(
            src_ref=src,
            dst_ref=dst,
            send_sem=send_sem.at[channel],
            recv_sem=arrived,
            device_id=peer,
            device_id_type=MESH,
        ).start()

    def over_sub(channel, src_of, dst, arrived_of=None):
        for step in far_first:
            peer = lax.rem(me_s + step, n_sub)
            arrived = recv_sem.at[channel] if arrived_of is None else arrived_of(step)
            send(src_of(peer), dst, channel, arrived, (me_g, peer))

    def over_group(channel, src_of, dst):
        for step in range(1, n_group):
            peer = lax.rem(me_g + step, n_group)
            send(src_of(peer), dst, channel, recv_sem.at[channel], (peer, me_s))

    def arrive(channel, part):
        pltpu.make_async_copy(part, part, recv_sem.at[channel]).wait()
        sent.append((channel, part))

    def message(phase):
        return pl.ds(0, half if phase == 0 else half + DOTS)

    def send_coarse(phase, part, dots):
        group_out[phase, 0] = jnp.concatenate([part[:half], dots], axis=0)
        group_out[phase, 1] = jnp.concatenate([part[half:], dots], axis=0)
        group_buf[phase, me_g] = group_out[phase, core]
        if phase == 0:
            pl.semaphore_wait(barrier, n_group - 1 + n_sub - 1)
        over_group(
            2 + phase,
            lambda peer: group_out.at[phase, lax.rem(peer, 2), message(phase)],
            group_buf.at[phase, me_g, message(phase)],
        )

    load(9).wait()
    load(0).wait()
    resid = rs_ref[...]
    send_coarse(0, mm(basis_ref[...], resid), jnp.zeros((SUBLANES, n_rhs), jnp.float32))

    for i in (4, 5, 6, 7):
        load(i).wait()
    slot = lax.broadcasted_iota(jnp.int32, (1, n_slots), 1)
    slot_peer = lax.broadcasted_iota(jnp.int32, (n_sub, n_slots), 1) // per_peer
    peer_ids = lax.broadcasted_iota(jnp.int32, (n_sub, n_slots), 0)
    of_peer = jnp.where(slot_peer == peer_ids, jnp.float32(1.0), jnp.float32(0.0))
    count_row = mm(
        jnp.broadcast_to(counts_ref[...].astype(jnp.float32), (SUBLANES, n_sub)), of_peer
    )[0:1]
    in_peer = (slot % per_peer).astype(jnp.float32)
    weights = jnp.where(in_peer < count_row - 0.5, fweight_ref[...], jnp.float32(0.0))
    row_ids = lax.broadcasted_iota(jnp.int32, (n_rows, n_slots), 0)
    face_hot = jnp.where(row_ids == faces_ref[...], weights, jnp.float32(0.0))
    land_hot = jnp.where(row_ids == lands_ref[...], jnp.float32(1.0), jnp.float32(0.0))
    spread = jnp.concatenate([land_hot, face_hot], axis=1)
    keep(spread_pair, spread)
    select = jnp.concatenate([face_hot, land_hot], axis=1).T
    keep(select_pair, select)

    weight_out[...] = mm(
        select[:n_slots, :], jnp.ones((n_rows, n_rhs), jnp.float32)
    ).reshape(n_sub, per_peer, n_rhs)
    weight_in[pl.ds(me_s, 1)] = weight_out[pl.ds(me_s, 1)]
    over_sub(0, lambda peer: weight_out.at[peer], weight_in.at[me_s])

    def gather_group(phase):
        arrive(2 + phase, group_buf.at[phase, pl.ds(0, n_group - 1), message(phase)])
        total = group_buf[phase, 0, message(phase)]
        for g in range(1, n_group):
            total = total + group_buf[phase, g, message(phase)]
        sub_buf[phase, core, me_s, message(phase)] = total
        mine = sub_buf.at[phase, core, me_s, message(phase)]
        over_sub(6 + phase, lambda peer: mine, mine, lambda step: step_sem.at[phase, step])
        forward(phase, me_s)

    def forward(phase, slot_of):
        part = sub_buf.at[phase, core, slot_of, pl.ds(0, half)]
        send(part, part, 13 + phase, recv_sem.at[13 + phase], (sibling, me_s))

    def keep_solve(rows_of, rows):
        for part in range(2):
            columns = slice(part * (total_coarse // 2), (part + 1) * (total_coarse // 2))
            keep(solve_pair.at[part], rows_of[:, columns], rows)

    gather_group(0)

    load(10).wait()
    basis_t = basis_ref[...].T
    keep(basis_t_pair, basis_t)
    keep(basis_pair, basis_ref[...])
    by_row = coarse_ref[...].T.reshape(n_sub, n_coarse, n_coarse)
    coarse = jnp.concatenate(
        [
            by_row[:, :half].reshape(total_coarse // 2, n_coarse),
            by_row[:, half:].reshape(total_coarse // 2, n_coarse),
        ],
        axis=0,
    ).T
    keep_solve(coarse, slice(0, n_coarse))
    load(8).wait()
    for i in range(n_factors):
        rows = slice(i * factor_rows, (i + 1) * factor_rows)
        part = factor_ref[rows, :]
        keep(near_pair, mm(part.T, part), rows)

    load(2).wait()
    load(3).wait()
    n_tiles = n_rows // LANES
    stored = n_stored * block_rows
    stored_tiles = stored // LANES
    stored_ids = lax.broadcasted_iota(jnp.int32, (n_stored, stored), 0)
    lane_block = lax.broadcasted_iota(jnp.int32, (n_stored, stored), 1) // block_rows
    of_stored = jnp.where(stored_ids == lane_block, jnp.float32(1.0), jnp.float32(0.0))
    wide_cols = mm(cols_ref[...].astype(jnp.float32), of_stored)
    high = lax.broadcasted_iota(jnp.int32, (1, LANES), 1) // block_rows
    row_sums = mm(values_ref[...], jnp.ones((n_stored * block_rows, n_rhs), jnp.float32))
    col_parts = jnp.concatenate(
        [
            jnp.sum(values_ref[b * block_rows : (b + 1) * block_rows, :], axis=0, keepdims=True)
            for b in range(n_blocks)
        ],
        axis=0,
    )
    col_sums = [jnp.zeros((n_blocks, LANES), jnp.float32) for _ in range(n_tiles)]
    for t in range(stored_tiles):
        tile = col_parts[:, t * LANES : (t + 1) * LANES]
        turned = pltpu.roll(tile, block_rows, 1)
        straight_cols = wide_cols[:, t * LANES : (t + 1) * LANES]
        turned_cols = pltpu.roll(straight_cols, block_rows, 1)
        for u in range(n_tiles):
            target = (2 * u + high).astype(jnp.float32)
            col_sums[u] = (
                col_sums[u]
                + jnp.where(jnp.abs(straight_cols - target) < 0.5, tile, jnp.float32(0.0))
                + jnp.where(jnp.abs(turned_cols - target) < 0.5, turned, jnp.float32(0.0))
            )
    col_row = jnp.concatenate(
        [jnp.sum(part, axis=0, keepdims=True) for part in col_sums], axis=1
    )
    load(1).wait()
    mass_col = jnp.broadcast_to(mass_ref[...] + col_row, (n_rhs, n_rows)).T
    arrive(0, weight_in.at[pl.ds(0, n_sub - 1)])
    degree = row_sums + mm(
        spread,
        jnp.concatenate(
            [
                weight_in[...].reshape(n_slots, n_rhs),
                jnp.ones((n_slots, n_rhs), jnp.float32),
            ],
            axis=0,
        ),
    )
    diag[...] = mass_col + degree
    inv_diag[...] = 1.0 / diag[...]

    def local_of(field, pair):
        parts = []
        for i in range(n_factors):
            rows = slice(i * factor_rows, (i + 1) * factor_rows)
            parts.append(mm3(near_pair, (pair[0][rows], pair[1][rows]), rows))
        return field * inv_diag[...] + jnp.concatenate(parts, axis=0)

    def send_faces(phase, field):
        picked = mm3(select_pair, split(field))
        face_out[phase, :, :per_peer, :] = picked[:n_slots].reshape(n_sub, per_peer, n_rhs)
        face_out[phase, :, per_peer:, :] = picked[n_slots:].reshape(n_sub, per_peer, n_rhs)
        face_in[phase, me_s] = face_out[phase, me_s]
        over_sub(10 + phase, lambda peer: face_out.at[phase, peer], face_in.at[phase, me_s])

    def receive(phase, local_part):
        if phase == 1:
            arrive(1, extend_in.at[pl.ds(0, n_sub - 1)])
            keep_solve(
                extend_in[...].reshape(2 * n_slots, total_coarse),
                slice(n_coarse, n_coarse + 2 * n_slots),
            )
        for step in reversed(far_first):
            origin = lax.rem(me_s + n_sub - step, n_sub)
            part = sub_buf.at[phase, core, origin, message(phase)]
            pltpu.make_async_copy(part, part, step_sem.at[phase, step]).wait()
            forward(phase, origin)
        dots = None if phase == 0 else jnp.sum(sub_buf[phase, core, :, half : half + DOTS, :], axis=0)
        sent.append((6 + phase, sub_buf.at[phase, 0, pl.ds(0, n_sub - 1), message(phase)]))
        rows = slice(0, n_coarse if phase == 0 else n_coarse + 2 * n_slots)

        def solve_half(part):
            gathered = sub_buf[phase, part, :, :half, :].reshape(total_coarse // 2, n_rhs)
            return mm3(solve_pair.at[part], split(gathered), rows)

        solved = solve_half(core)
        arrive(13 + phase, sub_buf.at[phase, 0, :, pl.ds(0, half)])
        solved = solved + solve_half(1 - core)
        if phase == 0:
            return local_part + mm3(basis_t_pair, split(solved)), None, None
        field = local_part + mm3(basis_t_pair, split(solved[:n_coarse]))
        return field, receive_faces(phase, solved[n_coarse:]), dots

    def receive_faces(phase, solved):
        arrive(10 + phase, face_in.at[phase, pl.ds(0, n_sub - 1)])
        far = face_in[phase]
        if solved is not None:
            far = far + solved.reshape(n_sub, 2 * per_peer, n_rhs)
        return jnp.concatenate(
            [
                far[:, :per_peer, :].reshape(n_slots, n_rhs),
                far[:, per_peer:, :].reshape(n_slots, n_rhs),
            ],
            axis=0,
        )

    def operate(field, far):
        pair = split(field)
        held_field = pair[0].astype(jnp.float32) + pair[1].astype(jnp.float32)
        return diag[...] * held_field - mm3(dense_pair, pair) - mm3(spread_pair, split(far))

    z, _, _ = receive(0, local_of(resid, split(resid)))
    send_faces(0, z)
    reach = mm(mm(select, basis_t), coarse)
    extend_out[:, :per_peer, :] = reach[:n_slots].reshape(n_sub, per_peer, total_coarse)
    extend_out[:, per_peer:, :] = reach[n_slots:].reshape(n_sub, per_peer, total_coarse)
    extend_in[pl.ds(me_s, 1)] = extend_out[pl.ds(me_s, 1)]
    over_sub(1, lambda peer: extend_out.at[peer], extend_in.at[me_s])

    for b in range(n_blocks):
        rows = slice(b * block_rows, (b + 1) * block_rows)
        sums = [jnp.zeros((block_rows, LANES), jnp.float32) for _ in range(n_tiles)]
        for t in range(stored_tiles):
            tile = values_ref[rows, t * LANES : (t + 1) * LANES]
            turned = pltpu.roll(tile, block_rows, 1)
            straight_cols = wide_cols[b : b + 1, t * LANES : (t + 1) * LANES]
            turned_cols = pltpu.roll(straight_cols, block_rows, 1)
            for u in range(n_tiles):
                target = (2 * u + high).astype(jnp.float32)
                straight = jnp.abs(straight_cols - target) < 0.5
                swapped = jnp.abs(turned_cols - target) < 0.5
                sums[u] = (
                    sums[u]
                    + jnp.where(straight, tile, jnp.float32(0.0))
                    + jnp.where(swapped, turned, jnp.float32(0.0))
                )
        for u in range(n_tiles):
            dense[rows, u * LANES : (u + 1) * LANES] = sums[u]
    keep(dense_pair, dense[...] + dense[...].T)
    z_far = receive_faces(0, None)
    image = operate(z, z_far)
    pair = split(image)
    send_coarse(
        1, mm3(basis_pair, pair), stack_dots([column_dot(resid, z), column_dot(z, image)])
    )
    local_part = local_of(image, pair)
    send_faces(1, local_part)
    gather_group(1)
    m_image, m_far, dots = receive(1, local_part)
    gamma, bent = dots[0:1], dots[1:2]
    alpha = gamma / bent
    direction = z
    first_alpha = alpha
    resid = resid - alpha * image
    z = z - alpha * m_image
    z_far = z_far - alpha * m_far
    z_image = operate(z, z_far)
    pair = split(z_image)
    send_coarse(
        2,
        mm3(basis_pair, pair),
        stack_dots([column_dot(resid, z), column_dot(z, z_image), column_dot(z, image)]),
    )
    local_part = local_of(z_image, pair)
    send_faces(2, local_part)
    gather_group(2)
    answer = first_alpha * direction
    m_z_image, m_z_far, dots = receive(2, local_part)
    beta = dots[0:1] / gamma
    gamma = dots[0:1]
    bent = dots[1:2] + beta * (2.0 * dots[2:3] + beta * bent)
    alpha = gamma / bent
    last_z, last_beta, last_alpha = z, beta, alpha
    z_far = z_far - alpha * (m_z_far + beta * m_far)
    z = z - alpha * (m_z_image + beta * m_image)
    image = z_image + beta * image
    resid = resid - alpha * image
    z_image = operate(z, z_far)
    group_dots[me_g] = stack_dots(
        [column_dot(resid, z), column_dot(z, z_image), column_dot(z, image)]
    )
    over_group(5, lambda peer: group_dots.at[me_g], group_dots.at[me_g])
    direction = last_z + last_beta * direction
    answer = answer + last_alpha * direction
    arrive(5, group_dots.at[pl.ds(0, n_group - 1)])
    sub_dots[me_s] = jnp.sum(group_dots[...], axis=0)
    over_sub(9, lambda peer: sub_dots.at[me_s], sub_dots.at[me_s])
    arrive(9, sub_dots.at[pl.ds(0, n_sub - 1)])
    dots = jnp.sum(sub_dots[...], axis=0)
    beta = dots[0:1] / gamma
    gamma = dots[0:1]
    bent = dots[1:2] + beta * (2.0 * dots[2:3] + beta * bent)
    alpha = gamma / bent
    out_ref[0] = answer + alpha * (z + beta * direction)
    out_ref[1] = resid - alpha * (z_image + beta * image)

    for channel, part in sent:
        pltpu.make_async_copy(part, part, send_sem.at[channel]).wait()


def divide(both_ref, x_ref, r_ref, sem):
    copies = [
        pltpu.make_async_copy(both_ref.at[i], out, sem.at[i]) for i, out in enumerate((x_ref, r_ref))
    ]
    for copy in copies:
        copy.start()
    for copy in copies:
        copy.wait()


def local(n_group, n_sub, *args):
    right_side, face_rows = args[0], args[4]
    basis, coarse_inverse = args[9], args[10]
    n_rows, n_rhs = right_side.shape
    n_slots = face_rows.shape[1]
    per_peer = n_slots // n_sub
    n_coarse = basis.shape[0]
    total_coarse = coarse_inverse.shape[1]
    factor_rows = args[8].shape[1]
    f32 = jnp.float32
    bf16 = jnp.bfloat16
    vmem = pl.BlockSpec(memory_space=pltpu.VMEM)
    message = n_coarse // 2 + SUBLANES
    scratch = [pltpu.VMEM(arg.shape, arg.dtype) for arg in args]
    scratch += [
        pltpu.VMEM((n_rows, n_rows), f32),
        pltpu.VMEM((2, n_rows, n_rows), bf16),
        pltpu.VMEM((2, n_rows, factor_rows), bf16),
        pltpu.VMEM((n_rows, n_rhs), f32),
        pltpu.VMEM((n_rows, n_rhs), f32),
        pltpu.VMEM((2, n_coarse, n_rows), bf16),
        pltpu.VMEM((2, n_rows, n_coarse), bf16),
        pltpu.VMEM((2, 2 * n_slots, n_rows), bf16),
        pltpu.VMEM((2, n_rows, 2 * n_slots), bf16),
        pltpu.VMEM((2, 2, n_coarse + 2 * n_slots, total_coarse // 2), bf16),
        pltpu.VMEM((n_sub, 2 * per_peer, total_coarse), f32),
        pltpu.VMEM((n_sub, 2 * per_peer, total_coarse), f32),
        pltpu.VMEM((n_sub, per_peer, n_rhs), f32),
        pltpu.VMEM((n_sub, per_peer, n_rhs), f32),
        pltpu.VMEM((3, 2, message, n_rhs), f32),
        pltpu.VMEM((3, n_group, message, n_rhs), f32),
        pltpu.VMEM((3, 2, n_sub, message, n_rhs), f32),
        pltpu.VMEM((3, n_sub, 2 * per_peer, n_rhs), f32),
        pltpu.VMEM((3, n_sub, 2 * per_peer, n_rhs), f32),
        pltpu.VMEM((n_group, SUBLANES, n_rhs), f32),
        pltpu.VMEM((n_sub, SUBLANES, n_rhs), f32),
        pltpu.SemaphoreType.DMA((N_IN,)),
        pltpu.SemaphoreType.DMA((16,)),
        pltpu.SemaphoreType.DMA((16,)),
        pltpu.SemaphoreType.DMA((3, n_sub)),
    ]
    field = jax.ShapeDtypeStruct((2, n_rows, n_rhs), f32)
    both = pl.pallas_call(
        functools.partial(kernel, n_group, n_sub),
        out_shape=field,
        in_specs=[pl.BlockSpec(memory_space=pl.ANY)] * N_IN,
        out_specs=vmem,
        scratch_shapes=scratch,
        compiler_params=pltpu.CompilerParams(
            collective_id=0, has_side_effects=True, vmem_limit_bytes=56 * 1024 * 1024
        ),
    )(*args)
    half = jax.ShapeDtypeStruct((n_rows, n_rhs), f32)
    anywhere = pl.BlockSpec(memory_space=pl.ANY)
    return pl.pallas_call(
        divide,
        out_shape=(half, half),
        in_specs=[anywhere],
        out_specs=(anywhere, anywhere),
        scratch_shapes=[pltpu.SemaphoreType.DMA((2,))],
        compiler_params=pltpu.CompilerParams(vmem_limit_bytes=56 * 1024 * 1024),
    )(both)


def solution(mesh):
    n_group, n_sub = mesh.shape["group"], mesh.shape["sub"]
    rows = P(("group", "sub"), None)
    return jax.shard_map(
        functools.partial(local, n_group, n_sub),
        mesh=mesh,
        in_specs=(rows,) * 10 + (P("sub", None),),
        out_specs=(rows, rows),
        check_vma=False,
    )
```

```python
import functools

import jax
import jax.numpy as jnp
from jax import lax
from jax.experimental import pallas as pl
from jax.experimental.pallas import tpu as pltpu
from jax.sharding import PartitionSpec as P

HIGHEST = lax.Precision.HIGHEST
MESH = pl.DeviceIdType.MESH
LANES = 128
SUBLANES = 8
DOTS = 4


def mm(a, b):
    return jnp.dot(a, b, precision=HIGHEST, preferred_element_type=jnp.float32)


def stack_dots(rows):
    pad = SUBLANES - len(rows)
    return jnp.concatenate(rows + [jnp.zeros((pad, rows[0].shape[1]), jnp.float32)], axis=0)


def column_dot(a, b):
    return jnp.sum(a * b, axis=0, keepdims=True)


def split(x):
    high = x.astype(jnp.bfloat16)
    low = (x - high.astype(jnp.float32)).astype(jnp.bfloat16)
    return high, low


def keep(pair_ref, x, rows=slice(None)):
    high, low = split(x)
    pair_ref[0, rows] = high
    pair_ref[1, rows] = low


def mm3(pair_ref, b, rows=slice(None)):
    high, low = b
    n = high.shape[1]
    wide = jnp.dot(
        pair_ref[0, rows], jnp.concatenate([high, low], axis=1), preferred_element_type=jnp.float32
    )
    cross = jnp.dot(pair_ref[1, rows], high, preferred_element_type=jnp.float32)
    return wide[:, :n] + (wide[:, n:] + cross)


N_IN = 11


def kernel(n_group, n_sub, *refs):
    hbm = refs[:N_IN]
    out_ref = refs[N_IN]
    held = refs[N_IN + 1 : 2 * N_IN + 1]
    (
        dense,
        dense_pair,
        near_pair,
        inv_diag,
        diag,
        basis_pair,
        basis_t_pair,
        select_pair,
        spread_pair,
        solve_pair,
        extend_out,
        extend_in,
        weight_out,
        weight_in,
        group_out,
        group_buf,
        sub_buf,
        face_out,
        face_in,
        group_dots,
        sub_dots,
        load_sem,
        send_sem,
        recv_sem,
        step_sem,
    ) = refs[2 * N_IN + 1 :]
    (
        rs_ref,
        mass_ref,
        values_ref,
        cols_ref,
        faces_ref,
        lands_ref,
        counts_ref,
        fweight_ref,
        factor_ref,
        basis_ref,
        coarse_ref,
    ) = held

    def load(i):
        return pltpu.make_async_copy(hbm[i], held[i], load_sem.at[i])

    for i in (9, 0, 4, 5, 6, 7, 10, 2, 3, 8, 1):
        load(i).start()

    me_g = lax.axis_index("group")
    me_s = lax.axis_index("sub")
    core = lax.rem(me_g, 2)
    sibling = me_g + 1 - 2 * core
    n_rows, n_rhs = rs_ref.shape
    n_slots = faces_ref.shape[1]
    per_peer = n_slots // n_sub
    n_blocks, n_stored = cols_ref.shape
    block_rows = n_rows // n_blocks
    n_coarse = basis_ref.shape[0]
    half = n_coarse // 2
    total_coarse = coarse_ref.shape[1]
    factor_rows = factor_ref.shape[1]
    n_factors = n_rows // factor_rows

    barrier = pltpu.get_barrier_semaphore()
    for step in range(1, n_group):
        peer = lax.rem(me_g + step, n_group)
        pl.semaphore_signal(barrier, inc=1, device_id=(peer, me_s), device_id_type=MESH)
    for step in range(1, n_sub):
        peer = lax.rem(me_s + step, n_sub)
        pl.semaphore_signal(barrier, inc=1, device_id=(me_g, peer), device_id_type=MESH)

    sent = []
    far_first = sorted(range(1, n_sub), key=lambda step: abs(step - n_sub // 2))

    def send(src, dst, channel, arrived, peer):
        pltpu.make_async_remote_copy(
            src_ref=src,
            dst_ref=dst,
            send_sem=send_sem.at[channel],
            recv_sem=arrived,
            device_id=peer,
            device_id_type=MESH,
        ).start()

    def over_sub(channel, src_of, dst, arrived_of=None):
        for step in far_first:
            peer = lax.rem(me_s + step, n_sub)
            arrived = recv_sem.at[channel] if arrived_of is None else arrived_of(step)
            send(src_of(peer), dst, channel, arrived, (me_g, peer))

    def over_group(channel, src_of, dst):
        for step in range(1, n_group):
            peer = lax.rem(me_g + step, n_group)
            send(src_of(peer), dst, channel, recv_sem.at[channel], (peer, me_s))

    def arrive(channel, part):
        pltpu.make_async_copy(part, part, recv_sem.at[channel]).wait()
        sent.append((channel, part))

    def message(phase):
        return pl.ds(0, half if phase == 0 else half + DOTS)

    def send_coarse(phase, part, dots):
        group_out[phase, 0] = jnp.concatenate([part[:half], dots], axis=0)
        group_out[phase, 1] = jnp.concatenate([part[half:], dots], axis=0)
        group_buf[phase, me_g] = group_out[phase, core]
        if phase == 0:
            pl.semaphore_wait(barrier, n_group - 1 + n_sub - 1)
        over_group(
            2 + phase,
            lambda peer: group_out.at[phase, lax.rem(peer, 2), message(phase)],
            group_buf.at[phase, me_g, message(phase)],
        )

    load(9).wait()
    load(0).wait()
    resid = rs_ref[...]
    send_coarse(0, mm(basis_ref[...], resid), jnp.zeros((SUBLANES, n_rhs), jnp.float32))

    for i in (4, 5, 6, 7):
        load(i).wait()
    slot = lax.broadcasted_iota(jnp.int32, (1, n_slots), 1)
    slot_peer = lax.broadcasted_iota(jnp.int32, (n_sub, n_slots), 1) // per_peer
    peer_ids = lax.broadcasted_iota(jnp.int32, (n_sub, n_slots), 0)
    of_peer = jnp.where(slot_peer == peer_ids, jnp.float32(1.0), jnp.float32(0.0))
    count_row = mm(
        jnp.broadcast_to(counts_ref[...].astype(jnp.float32), (SUBLANES, n_sub)), of_peer
    )[0:1]
    in_peer = (slot % per_peer).astype(jnp.float32)
    weights = jnp.where(in_peer < count_row - 0.5, fweight_ref[...], jnp.float32(0.0))
    row_ids = lax.broadcasted_iota(jnp.int32, (n_rows, n_slots), 0)
    face_hot = jnp.where(row_ids == faces_ref[...], weights, jnp.float32(0.0))
    land_hot = jnp.where(row_ids == lands_ref[...], jnp.float32(1.0), jnp.float32(0.0))
    spread = jnp.concatenate([land_hot, face_hot], axis=1)
    keep(spread_pair, spread)
    select = jnp.concatenate([face_hot, land_hot], axis=1).T
    keep(select_pair, select)

    weight_out[...] = mm(
        select[:n_slots, :], jnp.ones((n_rows, n_rhs), jnp.float32)
    ).reshape(n_sub, per_peer, n_rhs)
    weight_in[pl.ds(me_s, 1)] = weight_out[pl.ds(me_s, 1)]
    over_sub(0, lambda peer: weight_out.at[peer], weight_in.at[me_s])

    def gather_group(phase):
        arrive(2 + phase, group_buf.at[phase, pl.ds(0, n_group - 1), message(phase)])
        total = group_buf[phase, 0, message(phase)]
        for g in range(1, n_group):
            total = total + group_buf[phase, g, message(phase)]
        sub_buf[phase, core, me_s, message(phase)] = total
        mine = sub_buf.at[phase, core, me_s, message(phase)]
        over_sub(6 + phase, lambda peer: mine, mine, lambda step: step_sem.at[phase, step])
        forward(phase, me_s)

    def forward(phase, slot_of):
        part = sub_buf.at[phase, core, slot_of, pl.ds(0, half)]
        send(part, part, 13 + phase, recv_sem.at[13 + phase], (sibling, me_s))

    def keep_solve(rows_of, rows):
        for part in range(2):
            columns = slice(part * (total_coarse // 2), (part + 1) * (total_coarse // 2))
            keep(solve_pair.at[part], rows_of[:, columns], rows)

    gather_group(0)

    load(10).wait()
    basis_t = basis_ref[...].T
    keep(basis_t_pair, basis_t)
    keep(basis_pair, basis_ref[...])
    by_row = coarse_ref[...].T.reshape(n_sub, n_coarse, n_coarse)
    coarse = jnp.concatenate(
        [
            by_row[:, :half].reshape(total_coarse // 2, n_coarse),
            by_row[:, half:].reshape(total_coarse // 2, n_coarse),
        ],
        axis=0,
    ).T
    keep_solve(coarse, slice(0, n_coarse))
    load(8).wait()
    for i in range(n_factors):
        rows = slice(i * factor_rows, (i + 1) * factor_rows)
        part = factor_ref[rows, :]
        keep(near_pair, mm(part.T, part), rows)

    load(2).wait()
    load(3).wait()
    n_tiles = n_rows // LANES
    stored = n_stored * block_rows
    stored_tiles = stored // LANES
    stored_ids = lax.broadcasted_iota(jnp.int32, (n_stored, stored), 0)
    lane_block = lax.broadcasted_iota(jnp.int32, (n_stored, stored), 1) // block_rows
    of_stored = jnp.where(stored_ids == lane_block, jnp.float32(1.0), jnp.float32(0.0))
    wide_cols = mm(cols_ref[...].astype(jnp.float32), of_stored)
    high = lax.broadcasted_iota(jnp.int32, (1, LANES), 1) // block_rows
    row_sums = mm(values_ref[...], jnp.ones((n_stored * block_rows, n_rhs), jnp.float32))
    col_parts = jnp.concatenate(
        [
            jnp.sum(values_ref[b * block_rows : (b + 1) * block_rows, :], axis=0, keepdims=True)
            for b in range(n_blocks)
        ],
        axis=0,
    )
    col_sums = [jnp.zeros((n_blocks, LANES), jnp.float32) for _ in range(n_tiles)]
    for t in range(stored_tiles):
        tile = col_parts[:, t * LANES : (t + 1) * LANES]
        turned = pltpu.roll(tile, block_rows, 1)
        straight_cols = wide_cols[:, t * LANES : (t + 1) * LANES]
        turned_cols = pltpu.roll(straight_cols, block_rows, 1)
        for u in range(n_tiles):
            target = (2 * u + high).astype(jnp.float32)
            col_sums[u] = (
                col_sums[u]
                + jnp.where(jnp.abs(straight_cols - target) < 0.5, tile, jnp.float32(0.0))
                + jnp.where(jnp.abs(turned_cols - target) < 0.5, turned, jnp.float32(0.0))
            )
    col_row = jnp.concatenate(
        [jnp.sum(part, axis=0, keepdims=True) for part in col_sums], axis=1
    )
    load(1).wait()
    mass_col = jnp.broadcast_to(mass_ref[...] + col_row, (n_rhs, n_rows)).T
    arrive(0, weight_in.at[pl.ds(0, n_sub - 1)])
    degree = row_sums + mm(
        spread,
        jnp.concatenate(
            [
                weight_in[...].reshape(n_slots, n_rhs),
                jnp.ones((n_slots, n_rhs), jnp.float32),
            ],
            axis=0,
        ),
    )
    diag[...] = mass_col + degree
    inv_diag[...] = 1.0 / diag[...]

    def local_of(field, pair):
        parts = []
        for i in range(n_factors):
            rows = slice(i * factor_rows, (i + 1) * factor_rows)
            parts.append(mm3(near_pair, (pair[0][rows], pair[1][rows]), rows))
        return field * inv_diag[...] + jnp.concatenate(parts, axis=0)

    def send_faces(phase, field):
        picked = mm3(select_pair, split(field))
        face_out[phase, :, :per_peer, :] = picked[:n_slots].reshape(n_sub, per_peer, n_rhs)
        face_out[phase, :, per_peer:, :] = picked[n_slots:].reshape(n_sub, per_peer, n_rhs)
        face_in[phase, me_s] = face_out[phase, me_s]
        over_sub(10 + phase, lambda peer: face_out.at[phase, peer], face_in.at[phase, me_s])

    def receive(phase, local_part):
        if phase == 1:
            arrive(1, extend_in.at[pl.ds(0, n_sub - 1)])
            keep_solve(
                extend_in[...].reshape(2 * n_slots, total_coarse),
                slice(n_coarse, n_coarse + 2 * n_slots),
            )
        for step in reversed(far_first):
            origin = lax.rem(me_s + n_sub - step, n_sub)
            part = sub_buf.at[phase, core, origin, message(phase)]
            pltpu.make_async_copy(part, part, step_sem.at[phase, step]).wait()
            forward(phase, origin)
        dots = None if phase == 0 else jnp.sum(sub_buf[phase, core, :, half : half + DOTS, :], axis=0)
        sent.append((6 + phase, sub_buf.at[phase, 0, pl.ds(0, n_sub - 1), message(phase)]))
        rows = slice(0, n_coarse if phase == 0 else n_coarse + 2 * n_slots)

        def solve_half(part):
            gathered = sub_buf[phase, part, :, :half, :].reshape(total_coarse // 2, n_rhs)
            return mm3(solve_pair.at[part], split(gathered), rows)

        solved = solve_half(core)
        arrive(13 + phase, sub_buf.at[phase, 0, :, pl.ds(0, half)])
        solved = solved + solve_half(1 - core)
        if phase == 0:
            return local_part + mm3(basis_t_pair, split(solved)), None, None
        field = local_part + mm3(basis_t_pair, split(solved[:n_coarse]))
        return field, receive_faces(phase, solved[n_coarse:]), dots

    def receive_faces(phase, solved):
        arrive(10 + phase, face_in.at[phase, pl.ds(0, n_sub - 1)])
        far = face_in[phase]
        if solved is not None:
            far = far + solved.reshape(n_sub, 2 * per_peer, n_rhs)
        return jnp.concatenate(
            [
                far[:, :per_peer, :].reshape(n_slots, n_rhs),
                far[:, per_peer:, :].reshape(n_slots, n_rhs),
            ],
            axis=0,
        )

    def operate(field, far):
        pair = split(field)
        held_field = pair[0].astype(jnp.float32) + pair[1].astype(jnp.float32)
        return diag[...] * held_field - mm3(dense_pair, pair) - mm3(spread_pair, split(far))

    z, _, _ = receive(0, local_of(resid, split(resid)))
    send_faces(0, z)
    reach = mm(mm(select, basis_t), coarse)
    extend_out[:, :per_peer, :] = reach[:n_slots].reshape(n_sub, per_peer, total_coarse)
    extend_out[:, per_peer:, :] = reach[n_slots:].reshape(n_sub, per_peer, total_coarse)
    extend_in[pl.ds(me_s, 1)] = extend_out[pl.ds(me_s, 1)]
    over_sub(1, lambda peer: extend_out.at[peer], extend_in.at[me_s])

    for b in range(n_blocks):
        rows = slice(b * block_rows, (b + 1) * block_rows)
        sums = [jnp.zeros((block_rows, LANES), jnp.float32) for _ in range(n_tiles)]
        for t in range(stored_tiles):
            tile = values_ref[rows, t * LANES : (t + 1) * LANES]
            turned = pltpu.roll(tile, block_rows, 1)
            straight_cols = wide_cols[b : b + 1, t * LANES : (t + 1) * LANES]
            turned_cols = pltpu.roll(straight_cols, block_rows, 1)
            for u in range(n_tiles):
                target = (2 * u + high).astype(jnp.float32)
                straight = jnp.abs(straight_cols - target) < 0.5
                swapped = jnp.abs(turned_cols - target) < 0.5
                sums[u] = (
                    sums[u]
                    + jnp.where(straight, tile, jnp.float32(0.0))
                    + jnp.where(swapped, turned, jnp.float32(0.0))
                )
        for u in range(n_tiles):
            dense[rows, u * LANES : (u + 1) * LANES] = sums[u]
    keep(dense_pair, dense[...] + dense[...].T)
    z_far = receive_faces(0, None)
    image = operate(z, z_far)
    pair = split(image)
    send_coarse(
        1, mm3(basis_pair, pair), stack_dots([column_dot(resid, z), column_dot(z, image)])
    )
    local_part = local_of(image, pair)
    send_faces(1, local_part)
    gather_group(1)
    m_image, m_far, dots = receive(1, local_part)
    gamma, bent = dots[0:1], dots[1:2]
    alpha = gamma / bent
    direction = z
    first_alpha = alpha
    resid = resid - alpha * image
    z = z - alpha * m_image
    z_far = z_far - alpha * m_far
    z_image = operate(z, z_far)
    pair = split(z_image)
    send_coarse(
        2,
        mm3(basis_pair, pair),
        stack_dots([column_dot(resid, z), column_dot(z, z_image), column_dot(z, image)]),
    )
    local_part = local_of(z_image, pair)
    send_faces(2, local_part)
    gather_group(2)
    answer = first_alpha * direction
    m_z_image, m_z_far, dots = receive(2, local_part)
    beta = dots[0:1] / gamma
    gamma = dots[0:1]
    bent = dots[1:2] + beta * (2.0 * dots[2:3] + beta * bent)
    alpha = gamma / bent
    last_z, last_beta, last_alpha = z, beta, alpha
    z_far = z_far - alpha * (m_z_far + beta * m_far)
    z = z - alpha * (m_z_image + beta * m_image)
    image = z_image + beta * image
    resid = resid - alpha * image
    z_image = operate(z, z_far)
    group_dots[me_g] = stack_dots(
        [column_dot(resid, z), column_dot(z, z_image), column_dot(z, image)]
    )
    over_group(5, lambda peer: group_dots.at[me_g], group_dots.at[me_g])
    direction = last_z + last_beta * direction
    answer = answer + last_alpha * direction
    arrive(5, group_dots.at[pl.ds(0, n_group - 1)])
    sub_dots[me_s] = jnp.sum(group_dots[...], axis=0)
    over_sub(9, lambda peer: sub_dots.at[me_s], sub_dots.at[me_s])
    arrive(9, sub_dots.at[pl.ds(0, n_sub - 1)])
    dots = jnp.sum(sub_dots[...], axis=0)
    beta = dots[0:1] / gamma
    gamma = dots[0:1]
    bent = dots[1:2] + beta * (2.0 * dots[2:3] + beta * bent)
    alpha = gamma / bent
    out_ref[0] = answer + alpha * (z + beta * direction)
    out_ref[1] = resid - alpha * (z_image + beta * image)

    for channel, part in sent:
        pltpu.make_async_copy(part, part, send_sem.at[channel]).wait()


def local(n_group, n_sub, *args):
    right_side, face_rows = args[0], args[4]
    basis, coarse_inverse = args[9], args[10]
    n_rows, n_rhs = right_side.shape
    n_slots = face_rows.shape[1]
    per_peer = n_slots // n_sub
    n_coarse = basis.shape[0]
    total_coarse = coarse_inverse.shape[1]
    factor_rows = args[8].shape[1]
    f32 = jnp.float32
    bf16 = jnp.bfloat16
    vmem = pl.BlockSpec(memory_space=pltpu.VMEM)
    message = n_coarse // 2 + SUBLANES
    scratch = [pltpu.VMEM(arg.shape, arg.dtype) for arg in args]
    scratch += [
        pltpu.VMEM((n_rows, n_rows), f32),
        pltpu.VMEM((2, n_rows, n_rows), bf16),
        pltpu.VMEM((2, n_rows, factor_rows), bf16),
        pltpu.VMEM((n_rows, n_rhs), f32),
        pltpu.VMEM((n_rows, n_rhs), f32),
        pltpu.VMEM((2, n_coarse, n_rows), bf16),
        pltpu.VMEM((2, n_rows, n_coarse), bf16),
        pltpu.VMEM((2, 2 * n_slots, n_rows), bf16),
        pltpu.VMEM((2, n_rows, 2 * n_slots), bf16),
        pltpu.VMEM((2, 2, n_coarse + 2 * n_slots, total_coarse // 2), bf16),
        pltpu.VMEM((n_sub, 2 * per_peer, total_coarse), f32),
        pltpu.VMEM((n_sub, 2 * per_peer, total_coarse), f32),
        pltpu.VMEM((n_sub, per_peer, n_rhs), f32),
        pltpu.VMEM((n_sub, per_peer, n_rhs), f32),
        pltpu.VMEM((3, 2, message, n_rhs), f32),
        pltpu.VMEM((3, n_group, message, n_rhs), f32),
        pltpu.VMEM((3, 2, n_sub, message, n_rhs), f32),
        pltpu.VMEM((3, n_sub, 2 * per_peer, n_rhs), f32),
        pltpu.VMEM((3, n_sub, 2 * per_peer, n_rhs), f32),
        pltpu.VMEM((n_group, SUBLANES, n_rhs), f32),
        pltpu.VMEM((n_sub, SUBLANES, n_rhs), f32),
        pltpu.SemaphoreType.DMA((N_IN,)),
        pltpu.SemaphoreType.DMA((16,)),
        pltpu.SemaphoreType.DMA((16,)),
        pltpu.SemaphoreType.DMA((3, n_sub)),
    ]
    field = jax.ShapeDtypeStruct((2, n_rows, n_rhs), f32)
    both = pl.pallas_call(
        functools.partial(kernel, n_group, n_sub),
        out_shape=field,
        in_specs=[pl.BlockSpec(memory_space=pl.ANY)] * N_IN,
        out_specs=vmem,
        scratch_shapes=scratch,
        compiler_params=pltpu.CompilerParams(
            collective_id=0, has_side_effects=True, vmem_limit_bytes=56 * 1024 * 1024
        ),
    )(*args)
    return both[0], both[1]


def solution(mesh):
    n_group, n_sub = mesh.shape["group"], mesh.shape["sub"]
    rows = P(("group", "sub"), None)
    return jax.shard_map(
        functools.partial(local, n_group, n_sub),
        mesh=mesh,
        in_specs=(rows,) * 10 + (P("sub", None),),
        out_specs=(rows, rows),
        check_vma=False,
    )
```
